32 devices in a mesh: ctx: 8 (over z, y), tp: 4 (over x, core).
Axes of the slice: x: 2, y: 2, z: 4, core: 2. Of those that a mesh axis runs over, the one named last changes fastest.
Arguments:
- queries: bfloat16 [1152, 3072], P('ctx', 'tp'), may hold values from -8 to 8
- keys: bfloat16 [1152, 3072], P('ctx', 'tp'), may hold values from -8 to 8
- values: bfloat16 [1152, 3072], P('ctx', 'tp'), may hold values from -6 to 6
- positions: int32 [1152], P('ctx'), may hold values from 0 to 1151, as said below
- lambda_vecs: float32 [4, 12, 128], P(None, 'tp'), may hold values from -0.6 to 0.6
- head_gain: float32 [3072], P('tp'), may hold values from 0.5 to 1.5
- out_weight: bfloat16 [3072, 5120], P('tp'), may hold values from -0.109375 to 0.109375
- residual: bfloat16 [1152, 5120], P('ctx', 'tp'), may hold values from -3 to 3
Outputs:
- mixed: bfloat16 [1152, 5120], P('ctx', 'tp')
The draws below stay inside these ranges and needn't reach their ends.
Inputs may be any that keep to these rules, and one draw needn't show every extreme that they name: Each aligned run of 72 rows holds 72 consecutive positions in increasing order; the runs' first positions are the multiples of 72, each once.
All inputs are finite; a program needn't handle non-finite values.
Results may differ from the reference program's by a relative error of at most 0.012.
Values may be sent and summed in bfloat16 or wider, within the bound.
A program may use at most 192 MiB of HBM per device.

```python
import math
import jax
import jax.numpy as jnp
from jax import lax

D = 5120
HEAD_DIM = 128
HEADS = 12
TOKENS = 1152
BLOCK = 72


def drawn_rows(key, salt):
    width = HEADS * 2 * HEAD_DIM
    local_key = jax.random.fold_in(key, salt)
    return jnp.clip(jax.random.normal(local_key, (TOKENS, width), jnp.float32), -6.0, 6.0)


def draw_queries(key, part):
    result = drawn_rows(key, 3)
    return result.astype(jnp.bfloat16)


def draw_keys(key, part):
    result = drawn_rows(key, 5)
    return result.astype(jnp.bfloat16)


def draw_positions(key, part):
    block_count = TOKENS // BLOCK
    order = jax.random.permutation(jax.random.fold_in(key, 23), block_count).astype(jnp.int32)
    row_index = jnp.arange(TOKENS, dtype=jnp.int32)
    return (order[row_index // BLOCK] * BLOCK + row_index % BLOCK).astype(jnp.int32)


def level_of(stream_key, dims, shards, least, high):
    def one(dim, shards_of):
        draws = jax.random.uniform(jax.random.fold_in(jax.random.fold_in(stream_key, 6), dim), (shards_of,), jnp.float32, least / len(shards), high / len(shards))
        return jnp.repeat(jnp.exp(draws), dims[dim] // shards_of).reshape((-1,) + (1,) * (len(dims) - dim - 1))

    factor_of = one(*shards[0])
    for cut in shards[1:]:
        factor_of = factor_of * one(*cut)
    return factor_of


def bell_draw(stream_key, extent, scale, limit, cuts=(), kind=jnp.bfloat16):
    level = level_of(stream_key, extent, cuts, -0.22, 0.18) if cuts else 1.0
    values = jax.random.normal(stream_key, extent, jnp.float32) * scale * level
    return jnp.minimum(jnp.maximum(values, -limit), limit).astype(kind)


def setup_inputs(seed: int = 0) -> dict:
    splits = jax.random.split(jax.random.key(seed), 9)
    queries = draw_queries(jax.random.fold_in(splits[8], 71), 0)
    keys = draw_keys(jax.random.fold_in(splits[8], 71), 0)
    values = bell_draw(splits[2], (TOKENS, HEADS * 2 * HEAD_DIM), 1.0, 6.0, ((0, 8), (1, 4)))
    positions = draw_positions(jax.random.fold_in(splits[8], 71), 0)
    lambda_vecs = bell_draw(splits[4], (4, HEADS, HEAD_DIM), 0.15, 0.6, ((1, 4),), jnp.float32)
    head_gain = jnp.clip(1.0 + 0.1 * jax.random.normal(splits[5], (HEADS * 2 * HEAD_DIM,), jnp.float32), 0.5, 1.5)
    out_weight = bell_draw(splits[6], (HEADS * 2 * HEAD_DIM, D), (HEADS * 2 * HEAD_DIM) ** -0.5, 0.109375, ((0, 4),))
    residual = bell_draw(splits[7], (TOKENS, D), 0.5, 3.0, ((0, 8), (1, 4)))
    return {"queries": queries, "keys": keys, "values": values, "positions": positions, "lambda_vecs": lambda_vecs, "head_gain": head_gain, "out_weight": out_weight, "residual": residual}


lambda_init = 0.2
out_factor = 0.8
norm_eps = 1e-05

def reference(queries, keys, values, positions, lambda_vecs, head_gain, out_weight, residual):
    score_scale = 1.0 / math.sqrt(HEAD_DIM)
    lambda_head = jnp.exp(lax.optimization_barrier(jnp.sum(lambda_vecs[0] * lambda_vecs[1], -1))) - jnp.exp(lax.optimization_barrier(jnp.sum(lambda_vecs[2] * lambda_vecs[3], -1))) + lambda_init
    key_heads = keys.reshape(TOKENS, HEADS, 2, HEAD_DIM).astype(jnp.float32)
    value_heads = values.reshape(TOKENS, HEADS, 2 * HEAD_DIM).astype(jnp.float32)
    gain_heads = head_gain.reshape(HEADS, 1, 2 * HEAD_DIM)
    query_block = math.gcd(TOKENS, 256)

    def one_block(block_index):
        start = (block_index * query_block).astype(jnp.int32)
        query_rows = lax.dynamic_slice_in_dim(queries, start, query_block, 0)
        query_rows = query_rows.reshape(query_block, HEADS, 2, HEAD_DIM).astype(jnp.float32)
        row_positions = lax.dynamic_slice_in_dim(positions, start, query_block, 0)
        allowed = positions[None, :] <= row_positions[:, None]
        scores = jnp.einsum('ihad,jhad->ahij', query_rows, key_heads) * score_scale
        scores = jnp.where(allowed, scores, -jnp.inf)
        highest = lax.optimization_barrier(jnp.max(scores, -1, keepdims=True))
        expo = jnp.where(allowed, jnp.exp(scores - highest), 0.0)
        total = lax.optimization_barrier(jnp.sum(expo, -1))
        weights = expo.astype(jnp.bfloat16).astype(jnp.float32)
        attn = jnp.einsum('ahij,jhe->ahie', weights, value_heads) / total[..., None]
        diff = attn[0] - lambda_head[:, None, None] * attn[1]
        mean_square = lax.optimization_barrier(jnp.mean(diff * diff, -1, keepdims=True))
        normed = out_factor * diff / jnp.sqrt(mean_square + norm_eps) * gain_heads
        return jnp.transpose(normed, (1, 0, 2)).reshape(query_block, HEADS * 2 * HEAD_DIM).astype(jnp.bfloat16)
    normed_all = lax.map(one_block, jnp.arange(TOKENS // query_block, dtype=jnp.int32))
    normed_all = normed_all.reshape(TOKENS, HEADS * 2 * HEAD_DIM)
    projected = jnp.dot(normed_all, out_weight, preferred_element_type=jnp.float32)
    return (projected + residual.astype(jnp.float32)).astype(jnp.bfloat16)
```

```python
import functools
import math

import jax
import jax.numpy as jnp
from jax import lax
from jax.experimental import pallas as pl
from jax.experimental.pallas import tpu as pltpu
from jax.sharding import PartitionSpec as P

lambda_init = 0.2
out_factor = 0.8
norm_eps = 1e-05
MASKED = -3e38
LOWEST = -1e30
CHUNK = 256


def layer_kernel(
    n_ctx,
    n_tp,
    q_in,
    k_in,
    v_in,
    pos_in,
    lam_in,
    gain_in,
    w_in,
    out_ref,
    q_buf,
    kv_buf,
    pos_all,
    lam_buf,
    gain_buf,
    lam_wide,
    gain_wide,
    high,
    total,
    acc,
    stage,
    normed,
    w_buf,
    part,
    got,
    init_send,
    init_recv,
    small_send,
    small_recv,
    pos_send,
    pos_recv,
    line_send,
    line_recv,
    sib_send,
    sib_recv,
    o_send,
    o_recv,
    w_local,
    w_send,
    w_recv,
    p_send,
    p_recv,
):
    heads, rows, wide = q_buf.shape
    depth = wide // 2
    W = n_ctx // 2
    X = n_tp // 2
    n_chunk = w_buf.shape[1]
    scale = 1.0 / math.sqrt(depth)
    ctx = lax.axis_index("ctx")
    tp = lax.axis_index("tp")
    w, y = lax.div(ctx, 2), lax.rem(ctx, 2)
    x, c = lax.div(tp, 2), lax.rem(tp, 2)
    crossed = c != y
    straight = c == y

    def dev(a, b):
        return {"ctx": a, "tp": b}

    def remote(src, dst, send, recv, to):
        return pltpu.make_async_remote_copy(
            src_ref=src, dst_ref=dst, send_sem=send, recv_sem=recv, device_id=to, device_id_type=pl.DeviceIdType.MESH
        )

    partner = dev(2 * w + c, 2 * x + y)
    sibling = dev(ctx, 2 * x + 1 - c)

    barrier = pltpu.get_barrier_semaphore()

    def greet(to):
        pl.semaphore_signal(barrier, inc=1, device_id=to, device_id_type=pl.DeviceIdType.MESH)

    greet(sibling)

    @pl.when(crossed)
    def _():
        greet(partner)

    for i in range(1, X):
        greet(dev(ctx, 2 * lax.rem(x + i, X) + c))

    def greet_row(i, _):
        greet(dev(lax.rem(ctx + i, n_ctx), tp))
        return 0

    lax.fori_loop(1, n_ctx, greet_row, 0)
    pl.semaphore_wait(barrier, n_ctx - 1 + 1 + X - 1 + lax.rem(c + y, 2))

    def init_pairs(h):
        cols = pl.ds(h * wide, wide)
        return (
            (k_in.at[:, cols], kv_buf.at[h, w, y, :, pl.ds(0, wide)]),
            (v_in.at[:, cols], kv_buf.at[h, w, y, :, pl.ds(wide, wide)]),
            (q_in.at[:, cols], q_buf.at[h]),
        )

    small_pairs = ((lam_in, lam_buf), (gain_in, gain_buf))

    @pl.when(straight)
    def _():
        for h in range(heads):
            for j, (src, dst) in enumerate(init_pairs(h)):
                pltpu.make_async_copy(src, dst, init_recv.at[h, j]).start()
        for j, (src, dst) in enumerate(small_pairs):
            pltpu.make_async_copy(src, dst, small_recv.at[j]).start()

    @pl.when(crossed)
    def _():
        for h in range(heads):
            for j, (src, dst) in enumerate(init_pairs(h)):
                remote(src, dst, init_send.at[h, j], init_recv.at[h, j], partner).start()
        for j, (src, dst) in enumerate(small_pairs):
            remote(src, dst, small_send.at[j], small_recv.at[j], partner).start()

    def pos_copy(i):
        return remote(
            pos_in,
            pos_all.at[ctx],
            pos_send.at[i],
            pos_recv.at[ctx],
            dev(lax.rem(ctx + i, n_ctx), tp),
        )

    def pos_start(i, _):
        pos_copy(i).start()
        return 0

    lax.fori_loop(1, n_ctx, pos_start, 0)
    pos_all[ctx] = pos_in[...]

    col_count = n_chunk * CHUNK
    w_rows = heads * wide

    def w_src(i, j, core):
        start = pl.multiple_of((2 * i + core) * col_count + j * CHUNK, CHUNK)
        return w_in.at[:, pl.ds(start, CHUNK)]

    def w_dst(i, j):
        return w_buf.at[i, j, pl.ds(pl.multiple_of(c * w_rows, 16), w_rows)]

    def w_own(i, j):
        return pltpu.make_async_copy(w_src(i, j, c), w_dst(i, j), w_local.at[i, j])

    def w_give(i, j):
        return remote(w_src(i, j, 1 - c), w_dst(i, j), w_send.at[i, j], w_recv.at[i, j], sibling)

    def w_take(i, j):
        dst = w_buf.at[i, j, pl.ds(pl.multiple_of((1 - c) * w_rows, 16), w_rows)]
        return remote(w_src(i, j, c), dst, w_send.at[i, j], w_recv.at[i, j], sibling)

    def line_copy(h, idx, way):
        block = kv_buf.at[h, idx, c]
        to = dev(ctx + (2 if way else -2), tp)
        return remote(block, block, line_send.at[way, h, idx], line_recv.at[h, idx], to)

    def sib_copy(h, idx):
        block = kv_buf.at[h, idx, c]
        return remote(block, block, sib_send.at[h, idx], sib_recv.at[h, idx], sibling)

    def sib_wait(h, idx):
        block = kv_buf.at[h, idx, 1 - c]
        remote(block, block, sib_send.at[h, idx], sib_recv.at[h, idx], sibling).wait_recv()

    def attend(h, idx):
        q_pos = high_q()
        k_pos = jnp.concatenate([pos_all[2 * idx], pos_all[2 * idx + 1]], axis=1)
        allowed = k_pos <= q_pos
        value = kv_buf[h, idx, :, :, pl.ds(wide, wide)].reshape(2 * rows, wide)
        for a in range(2):
            query = q_buf[h, :, pl.ds(a * depth, depth)]
            key = kv_buf[h, idx, :, :, pl.ds(a * depth, depth)].reshape(2 * rows, depth)
            scores = (
                lax.dot_general(query, key, (((1,), (1,)), ((), ())), preferred_element_type=jnp.float32) * scale
            )
            scores = jnp.where(allowed, scores, MASKED)
            before = high[h, a]
            now = jnp.maximum(before, jnp.max(scores, -1, keepdims=True))
            keep = jnp.exp(before - now)
            expo = jnp.exp(scores - now)
            high[h, a] = now
            total[h, a] = total[h, a] * keep + jnp.sum(expo, -1, keepdims=True)
            acc[h, a] = acc[h, a] * keep + jnp.dot(
                expo.astype(jnp.bfloat16), value, preferred_element_type=jnp.float32
            )

    def high_q():
        line = pos_all[2 * w + c]
        square = (rows, rows)
        same = lax.broadcasted_iota(jnp.int32, square, 0) == lax.broadcasted_iota(jnp.int32, square, 1)
        return jnp.sum(jnp.where(same, jnp.broadcast_to(line, square), 0), -1, keepdims=True)

    def o_copy(h, core):
        cols = pl.ds(pl.multiple_of((y * heads + h) * wide, wide), wide)
        return remote(
            stage.at[h], normed.at[:, cols], o_send.at[core, h], o_recv.at[y, h], dev(2 * w + c, 2 * x + core)
        )

    def o_wait(g, h):
        cols = pl.ds(pl.multiple_of((g * heads + h) * wide, wide), wide)
        remote(stage.at[h], normed.at[:, cols], o_send.at[0, h], o_recv.at[g, h], sibling).wait_recv()

    def finish(h):
        first = acc[h, 0] / total[h, 0]
        second = acc[h, 1] / total[h, 1]
        diff = first - lam_wide[h] * second
        mean_square = jnp.mean(diff * diff, -1, keepdims=True)
        result = (out_factor * diff * lax.rsqrt(mean_square + norm_eps) * gain_wide[h]).astype(jnp.bfloat16)
        stage[h] = result

        @pl.when(straight)
        def _():
            normed[:, pl.ds(pl.multiple_of((y * heads + h) * wide, wide), wide)] = result
            o_copy(h, 1 - c).start()

        @pl.when(crossed)
        def _():
            o_copy(h, 0).start()
            o_copy(h, 1).start()

    high[...] = jnp.full(high.shape, LOWEST, jnp.float32)
    total[...] = jnp.zeros(total.shape, jnp.float32)
    acc[...] = jnp.zeros(acc.shape, jnp.float32)

    def step(t, _):
        s, h = lax.div(t, heads), lax.rem(t, heads)

        @pl.when(s == 0)
        def _():
            cols = pl.ds(0, wide)
            src = k_in.at[:, cols]
            pltpu.make_async_copy(src, kv_buf.at[h, w, c, :, cols], init_recv.at[h, 0]).wait()
            pltpu.make_async_copy(src, kv_buf.at[h, w, c, :, pl.ds(wide, wide)], init_recv.at[h, 1]).wait()

            @pl.when(w > 0)
            def _():
                line_copy(h, w, 0).start()

            @pl.when(w < W - 1)
            def _():
                line_copy(h, w, 1).start()

            sib_copy(h, w).start()
            pltpu.make_async_copy(src, q_buf.at[h], init_recv.at[h, 2]).wait()

        @pl.when(t == heads)
        def _():
            for i in range(X):
                for j in range(n_chunk):
                    w_own(i, j).start()
                    w_give(i, j).start()
            for j, (src, dst) in enumerate(small_pairs):
                pltpu.make_async_copy(src, dst, small_recv.at[j]).wait()
            vecs = lam_buf[...]
            lam = (
                jnp.exp(jnp.sum(vecs[0] * vecs[1], -1, keepdims=True))
                - jnp.exp(jnp.sum(vecs[2] * vecs[3], -1, keepdims=True))
                + lambda_init
            )
            for i in range(heads):
                lam_wide[i] = jnp.broadcast_to(lam[i : i + 1], (1, wide))
                gain_wide[i] = gain_buf[:, pl.ds(i * wide, wide)]

        @pl.when((s > 0) & (s < W))
        def _():
            @pl.when(w - s >= 0)
            def _():
                line_copy(h, w - s, 1).wait_recv()

                @pl.when(w < W - 1)
                def _():
                    line_copy(h, w - s, 1).start()

                sib_copy(h, w - s).start()

            @pl.when(w + s < W)
            def _():
                line_copy(h, w + s, 0).wait_recv()

                @pl.when(w > 0)
                def _():
                    line_copy(h, w + s, 0).start()

                sib_copy(h, w + s).start()

        @pl.when(t == 1)
        def _():
            def pos_wait(i, _):
                frm = lax.rem(ctx + i, n_ctx)
                remote(pos_in, pos_all.at[frm], pos_send.at[i], pos_recv.at[frm], sibling).wait_recv()
                return 0

            lax.fori_loop(1, n_ctx, pos_wait, 0)

        @pl.when(t > 0)
        def _():
            s1, h1 = lax.div(t - 1, heads), lax.rem(t - 1, heads)

            @pl.when(w - s1 >= 0)
            def _():
                sib_wait(h1, w - s1)
                attend(h1, w - s1)

            @pl.when((s1 > 0) & (w + s1 < W))
            def _():
                sib_wait(h1, w + s1)
                attend(h1, w + s1)

            @pl.when(s1 == W - 1)
            def _():
                finish(h1)

        return 0

    lax.fori_loop(0, W * heads + 1, step, 0)

    for i in range(X):
        for j in range(n_chunk):
            w_own(i, j).wait()
            w_take(i, j).wait_recv()
    for h in range(heads):
        o_wait(1 - y, h)

        @pl.when(crossed)
        def _():
            o_wait(y, h)

    def product(i, j):
        return jnp.dot(normed[...], w_buf[i, j], preferred_element_type=jnp.float32)

    def p_copy(i, j):
        other = lax.rem(x + i, X)
        return remote(
            part.at[i - 1, j], got.at[i - 1, j], p_send.at[i - 1, j], p_recv.at[i - 1, j], dev(ctx, 2 * other + c)
        )

    for i in range(1, X):

        def send_chunk(j, _):
            part[i - 1, j] = product(lax.rem(x + i, X), j).astype(jnp.bfloat16)
            p_copy(i, j).start()
            return 0

        lax.fori_loop(0, n_chunk, send_chunk, 0)

    def own_chunk(j, _):
        out_ref[:, pl.ds(pl.multiple_of(j * CHUNK, CHUNK), CHUNK)] = product(x, j)
        return 0

    lax.fori_loop(0, n_chunk, own_chunk, 0)

    for i in range(X):
        for j in range(n_chunk):
            w_give(i, j).wait_send()

    def pos_done(i, _):
        pos_copy(i).wait_send()
        return 0

    lax.fori_loop(1, n_ctx, pos_done, 0)

    @pl.when(crossed)
    def _():
        for h in range(heads):
            for j, (src, dst) in enumerate(init_pairs(h)):
                remote(src, dst, init_send.at[h, j], init_recv.at[h, j], partner).wait_send()
            o_copy(h, 0).wait_send()
            o_copy(h, 1).wait_send()
        for j, (src, dst) in enumerate(small_pairs):
            remote(src, dst, small_send.at[j], small_recv.at[j], partner).wait_send()

    @pl.when(straight)
    def _():
        for h in range(heads):
            o_copy(h, 1 - c).wait_send()

    def line_done(idx, _):
        for h in range(heads):
            sib_copy(h, idx).wait_send()

            @pl.when((idx <= w) & (w < W - 1))
            def _():
                line_copy(h, idx, 1).wait_send()

            @pl.when((idx >= w) & (w > 0))
            def _():
                line_copy(h, idx, 0).wait_send()

        return 0

    lax.fori_loop(0, W, line_done, 0)

    for i in range(1, X):

        def add_chunk(j, _):
            p_copy(i, j).wait()
            cols = pl.ds(pl.multiple_of(j * CHUNK, CHUNK), CHUNK)
            out_ref[:, cols] += got[i - 1, j].astype(jnp.float32)
            return 0

        lax.fori_loop(0, n_chunk, add_chunk, 0)


def per_device(n_ctx, n_tp, queries, keys, values, positions, lambda_vecs, head_gain, out_weight, residual):
    rows = queries.shape[0]
    heads, depth = lambda_vecs.shape[1], lambda_vecs.shape[2]
    wide = 2 * depth
    W, X = n_ctx // 2, n_tp // 2
    columns = out_weight.shape[1] // n_tp
    n_chunk = columns // CHUNK
    vmem = pl.BlockSpec(memory_space=pltpu.VMEM)
    hbm = pl.BlockSpec(memory_space=pl.ANY)
    bf16, f32 = jnp.bfloat16, jnp.float32
    dma = pltpu.SemaphoreType.DMA
    projected = pl.pallas_call(
        functools.partial(layer_kernel, n_ctx, n_tp),
        out_shape=jax.ShapeDtypeStruct((rows, columns), f32),
        in_specs=[hbm, hbm, hbm, vmem, vmem, vmem, hbm],
        out_specs=vmem,
        scratch_shapes=[
            pltpu.VMEM((heads, rows, wide), bf16),
            pltpu.VMEM((heads, W, 2, rows, 2 * wide), bf16),
            pltpu.VMEM((n_ctx, 1, rows), jnp.int32),
            pltpu.VMEM(lambda_vecs.shape, f32),
            pltpu.VMEM((1, heads * wide), f32),
            pltpu.VMEM((heads, 1, wide), f32),
            pltpu.VMEM((heads, 1, wide), f32),
            pltpu.VMEM((heads, 2, rows, 1), f32),
            pltpu.VMEM((heads, 2, rows, 1), f32),
            pltpu.VMEM((heads, 2, rows, wide), f32),
            pltpu.VMEM((heads, rows, wide), bf16),
            pltpu.VMEM((rows, 2 * heads * wide), bf16),
            pltpu.VMEM((X, n_chunk, 2 * heads * wide, CHUNK), bf16),
            pltpu.VMEM((X - 1, n_chunk, rows, CHUNK), bf16),
            pltpu.VMEM((X - 1, n_chunk, rows, CHUNK), bf16),
            dma((heads, 3)),
            dma((heads, 3)),
            dma((2,)),
            dma((2,)),
            dma((n_ctx,)),
            dma((n_ctx,)),
            dma((2, heads, W)),
            dma((heads, W)),
            dma((heads, W)),
            dma((heads, W)),
            dma((2, heads)),
            dma((2, heads)),
            dma((X, n_chunk)),
            dma((X, n_chunk)),
            dma((X, n_chunk)),
            dma((X - 1, n_chunk)),
            dma((X - 1, n_chunk)),
        ],
        compiler_params=pltpu.CompilerParams(
            collective_id=0, has_side_effects=True, vmem_limit_bytes=56 * 1024 * 1024
        ),
        name="attend_and_project",
    )(
        queries,
        keys,
        values,
        positions.reshape(1, rows),
        lambda_vecs,
        head_gain.reshape(1, heads * wide),
        out_weight,
    )
    return (projected + residual.astype(f32)).astype(bf16)


def solution(mesh):
    placed = (
        P("ctx", "tp"),
        P("ctx", "tp"),
        P("ctx", "tp"),
        P("ctx"),
        P(None, "tp", None),
        P("tp"),
        P("tp", None),
        P("ctx", "tp"),
    )
    return jax.shard_map(
        functools.partial(per_device, mesh.shape["ctx"], mesh.shape["tp"]),
        mesh=mesh,
        in_specs=placed,
        out_specs=P("ctx", "tp"),
        check_vma=False,
    )
```

```python
import functools
import math

import jax
import jax.numpy as jnp
from jax import lax
from jax.experimental import pallas as pl
from jax.experimental.pallas import tpu as pltpu
from jax.sharding import PartitionSpec as P

lambda_init = 0.2
out_factor = 0.8
norm_eps = 1e-05
MASKED = -3e38
LOWEST = -1e30
CHUNK = 256


def layer_kernel(
    n_ctx,
    n_tp,
    q_in,
    k_in,
    v_in,
    pos_in,
    lam_in,
    gain_in,
    w_in,
    res_in,
    out_ref,
    q_buf,
    kv_buf,
    pos_all,
    lam_buf,
    gain_buf,
    lam_wide,
    gain_wide,
    q_pos,
    high,
    total,
    acc,
    stage,
    normed,
    w_buf,
    res_buf,
    part_sib,
    got_sib,
    part,
    got,
    init_send,
    init_recv,
    small_send,
    small_recv,
    pos_send,
    pos_recv,
    line_send,
    line_recv,
    sib_send,
    sib_recv,
    q_send,
    q_recv,
    o_send,
    o_recv,
    w_sem,
    res_sem,
    ps_send,
    ps_recv,
    p_send,
    p_recv,
):
    heads, rows, wide = stage.shape
    heads -= 1
    depth = wide // 2
    W = n_ctx // 2
    X = n_tp // 2
    n_chunk = w_buf.shape[1]
    off = heads - 1 if W >= 4 else -1
    scale = 1.0 / math.sqrt(depth)
    ctx = lax.axis_index("ctx")
    tp = lax.axis_index("tp")
    w, y = lax.div(ctx, 2), lax.rem(ctx, 2)
    x, c = lax.div(tp, 2), lax.rem(tp, 2)
    crossed = c != y
    straight = c == y
    at_end = (off >= 0) & ((w == 0) | (w == W - 1))
    helper = (off >= 0) & ((w == 1) | (w == W - 2))
    mate = jnp.where(w == 0, 1, jnp.where(w == W - 1, W - 2, jnp.where(w == 1, 0, jnp.where(w == W - 2, W - 1, w))))

    def left_out(h):
        return at_end & (h == off)

    def goes(way, h):
        if way:
            return (w < W - 1) & ((w != W - 2) | (h != off))
        return (w > 0) & ((w != 1) | (h != off))

    def slots(h):
        return 1 + jnp.where(helper & (h == off), 1, 0)

    def dev(a, b):
        return {"ctx": a, "tp": b}

    def remote(src, dst, send, recv, to):
        return pltpu.make_async_remote_copy(
            src_ref=src, dst_ref=dst, send_sem=send, recv_sem=recv, device_id=to, device_id_type=pl.DeviceIdType.MESH
        )

    partner = dev(2 * w + c, 2 * x + y)
    sibling = dev(ctx, 2 * x + 1 - c)
    far = dev(2 * mate + c, 2 * x + y)

    barrier = pltpu.get_barrier_semaphore()

    def greet(to):
        pl.semaphore_signal(barrier, inc=1, device_id=to, device_id_type=pl.DeviceIdType.MESH)

    greet(sibling)

    @pl.when(crossed)
    def _():
        greet(partner)

    @pl.when(crossed & (at_end | helper))
    def _():
        greet(far)

    for i in range(1, X):
        greet(dev(ctx, 2 * lax.rem(x + i, X) + c))

    def greet_row(i, _):
        greet(dev(lax.rem(ctx + i, n_ctx), tp))
        return 0

    lax.fori_loop(1, n_ctx, greet_row, 0)
    pl.semaphore_wait(barrier, n_ctx - 1 + 1 + X - 1 + lax.rem(c + y, 2) + jnp.where(crossed & (at_end | helper), 1, 0))

    def init_pairs(h):
        cols = pl.ds(h * wide, wide)
        return (
            (k_in.at[:, cols], kv_buf.at[h, w, y, :, pl.ds(0, wide)]),
            (v_in.at[:, cols], kv_buf.at[h, w, y, :, pl.ds(wide, wide)]),
            (q_in.at[:, cols], q_buf.at[h]),
        )

    small_pairs = ((lam_in, lam_buf), (gain_in, gain_buf))

    @pl.when(straight)
    def _():
        for h in range(heads):
            for j, (src, dst) in enumerate(init_pairs(h)):
                pltpu.make_async_copy(src, dst, init_recv.at[h, j]).start()
        for j, (src, dst) in enumerate(small_pairs):
            pltpu.make_async_copy(src, dst, small_recv.at[j]).start()

    @pl.when(crossed)
    def _():
        for h in range(heads):
            for j, (src, dst) in enumerate(init_pairs(h)):
                remote(src, dst, init_send.at[h, j], init_recv.at[h, j], partner).start()
        for j, (src, dst) in enumerate(small_pairs):
            remote(src, dst, small_send.at[j], small_recv.at[j], partner).start()

    def pos_copy(i):
        return remote(
            pos_in,
            pos_all.at[ctx],
            pos_send.at[i],
            pos_recv.at[ctx],
            dev(lax.rem(ctx + i, n_ctx), tp),
        )

    def pos_start(i, _):
        pos_copy(i).start()
        return 0

    pltpu.make_async_copy(pos_in, pos_all.at[ctx], pos_recv.at[ctx]).start()
    lax.fori_loop(1, n_ctx, pos_start, 0)

    def w_copy(i, j):
        start = pl.multiple_of((i * n_chunk + j) * CHUNK, CHUNK)
        return pltpu.make_async_copy(w_in.at[:, pl.ds(start, CHUNK)], w_buf.at[i, j], w_sem.at[i, j])

    res_copy = pltpu.make_async_copy(res_in, res_buf, res_sem)

    def line_copy(h, idx, way):
        block = kv_buf.at[h, idx, c]
        to = dev(ctx + (2 if way else -2), tp)
        return remote(block, block, line_send.at[way, h, idx], line_recv.at[h, idx], to)

    def sib_copy(h, idx):
        block = kv_buf.at[h, idx, c]
        return remote(block, block, sib_send.at[h, idx], sib_recv.at[h, idx], sibling)

    def sib_wait(h, idx):
        block = kv_buf.at[h, idx, 1 - c]
        remote(block, block, sib_send.at[h, idx], sib_recv.at[h, idx], sibling).wait_recv()

    def q_copy():
        return remote(q_buf.at[max(off, 0)], q_buf.at[heads], q_send, q_recv, dev(2 * mate + y, tp))

    def position_column(row):
        line = pos_all[row]
        square = (rows, rows)
        same = lax.broadcasted_iota(jnp.int32, square, 0) == lax.broadcasted_iota(jnp.int32, square, 1)
        return jnp.sum(jnp.where(same, jnp.broadcast_to(line, square), 0), -1, keepdims=True)

    def attend(h, idx):
        def one(k, _):
            e = h + k * (heads - h)
            k_pos = jnp.concatenate([pos_all[2 * idx], pos_all[2 * idx + 1]], axis=1)
            allowed = k_pos <= q_pos[k]
            value = kv_buf[h, idx, :, :, pl.ds(wide, wide)].reshape(2 * rows, wide)
            before = [high[e, a] for a in range(2)]
            sums = [total[e, a] for a in range(2)]
            held = [acc[e, a] for a in range(2)]
            for a in range(2):
                query = q_buf[e, :, pl.ds(a * depth, depth)]
                key = kv_buf[h, idx, :, :, pl.ds(a * depth, depth)].reshape(2 * rows, depth)
                scores = (
                    lax.dot_general(query, key, (((1,), (1,)), ((), ())), preferred_element_type=jnp.float32) * scale
                )
                scores = jnp.where(allowed, scores, MASKED)
                now = jnp.maximum(before[a], jnp.max(scores, -1, keepdims=True))
                keep = jnp.exp(before[a] - now)
                expo = jnp.exp(scores - now)
                before[a] = now
                sums[a] = sums[a] * keep + jnp.sum(expo, -1, keepdims=True)
                held[a] = held[a] * keep + jnp.dot(
                    expo.astype(jnp.bfloat16), value, preferred_element_type=jnp.float32
                )
            for a in range(2):
                high[e, a] = before[a]
                total[e, a] = sums[a]
                acc[e, a] = held[a]
            return 0

        lax.fori_loop(0, slots(h), one, 0)

    def head_columns(h):
        return pl.ds(pl.multiple_of(h * wide, wide), wide)

    def o_copy(h, k):
        e = h + k * (heads - h)
        to = dev(2 * (w + k * (mate - w)) + c, 2 * x + y)
        return remote(stage.at[e], normed.at[:, head_columns(h)], o_send.at[e], o_recv.at[h], to)

    def finish(h):
        def one(k, _):
            e = h + k * (heads - h)
            first = acc[e, 0] / total[e, 0]
            second = acc[e, 1] / total[e, 1]
            diff = first - lam_wide[h] * second
            mean_square = jnp.mean(diff * diff, -1, keepdims=True)
            result = (out_factor * diff * lax.rsqrt(mean_square + norm_eps) * gain_wide[h]).astype(jnp.bfloat16)

            @pl.when(straight & (k == 0))
            def _():
                normed[:, head_columns(h)] = result

            @pl.when(crossed | (k > 0))
            def _():
                stage[e] = result
                o_copy(h, k).start()

            return 0

        lax.fori_loop(0, slots(h), one, 0)

    for i in range(1, n_tp + 1):
        for j in range(n_chunk):
            w_copy(lax.rem(tp + i, n_tp), j).start()
    res_copy.start()

    high[...] = jnp.full(high.shape, LOWEST, jnp.float32)
    total[...] = jnp.zeros(total.shape, jnp.float32)
    acc[...] = jnp.zeros(acc.shape, jnp.float32)

    def step(t, _):
        s, h = lax.div(t, heads), lax.rem(t, heads)

        @pl.when(s == 0)
        def _():
            cols = pl.ds(0, wide)
            src = k_in.at[:, cols]
            pltpu.make_async_copy(src, kv_buf.at[h, w, c, :, cols], init_recv.at[h, 0]).wait()
            pltpu.make_async_copy(src, kv_buf.at[h, w, c, :, pl.ds(wide, wide)], init_recv.at[h, 1]).wait()

            for way in range(2):

                @pl.when(goes(way, h))
                def _():
                    line_copy(h, w, way).start()

            @pl.when(jnp.logical_not(left_out(h)))
            def _():
                sib_copy(h, w).start()

            pltpu.make_async_copy(src, q_buf.at[h], init_recv.at[h, 2]).wait()

            @pl.when(left_out(h))
            def _():
                q_copy().start()

        @pl.when(t == heads)
        def _():
            for j, (src, dst) in enumerate(small_pairs):
                pltpu.make_async_copy(src, dst, small_recv.at[j]).wait()
            vecs = lam_buf[...]
            lam = (
                jnp.exp(jnp.sum(vecs[:, 0] * vecs[:, 1], -1, keepdims=True))
                - jnp.exp(jnp.sum(vecs[:, 2] * vecs[:, 3], -1, keepdims=True))
                + lambda_init
            )
            for i in range(heads):
                lam_wide[i] = jnp.broadcast_to(lam[i : i + 1], (1, wide))
                gain_wide[i] = jnp.concatenate([gain_buf[pl.ds(2 * i, 1)], gain_buf[pl.ds(2 * i + 1, 1)]], axis=1)

        @pl.when((s > 0) & (s < W) & jnp.logical_not(left_out(h)))
        def _():
            for way, idx in ((1, w - s), (0, w + s)):

                @pl.when((idx >= 0) & (idx < W))
                def _():
                    line_copy(h, idx, way).wait_recv()

                    @pl.when(goes(way, h))
                    def _():
                        line_copy(h, idx, way).start()

                    sib_copy(h, idx).start()

        @pl.when(t == 1)
        def _():
            def pos_wait(i, _):
                frm = lax.rem(ctx + i, n_ctx)
                remote(pos_in, pos_all.at[frm], pos_send.at[i], pos_recv.at[frm], sibling).wait_recv()
                return 0

            pltpu.make_async_copy(pos_in, pos_all.at[ctx], pos_recv.at[ctx]).wait()
            lax.fori_loop(1, n_ctx, pos_wait, 0)
            q_pos[0] = position_column(2 * w + c)
            q_pos[1] = position_column(2 * mate + c)

        s1, h1 = lax.div(t + heads - 1, heads) - 1, lax.rem(t + heads - 1, heads)

        @pl.when((t > 0) & jnp.logical_not(left_out(h1)))
        def _():
            @pl.when(helper & (t == off + 1))
            def _():
                q_copy().wait_recv()

            @pl.when(w - s1 >= 0)
            def _():
                sib_wait(h1, w - s1)
                attend(h1, w - s1)

            @pl.when((s1 > 0) & (w + s1 < W))
            def _():
                sib_wait(h1, w + s1)
                attend(h1, w + s1)

            @pl.when(s1 == jnp.maximum(w, W - 1 - w))
            def _():
                finish(h1)

        return 0

    lax.fori_loop(0, W * heads + 1, step, 0)

    for h in range(heads):

        @pl.when(crossed | left_out(h))
        def _():
            o_copy(h, 0).wait_recv()

    def product(i, core, j):
        target = 2 * lax.rem(x + i, X) + core
        w_copy(target, j).wait()
        return jnp.dot(normed[...], w_buf[target, j], preferred_element_type=jnp.float32)

    def ps_copy(i, j):
        return remote(part_sib.at[i, j], got_sib.at[i, j], ps_send.at[i, j], ps_recv.at[i, j], sibling)

    def p_copy(i, j):
        to = dev(ctx, 2 * lax.rem(x + i, X) + c)
        return remote(part.at[i - 1, j], got.at[i - 1, j], p_send.at[i - 1, j], p_recv.at[i - 1, j], to)

    def give_sibling(i):
        def body(j, _):
            part_sib[i, j] = product(i, 1 - c, j).astype(jnp.bfloat16)
            ps_copy(i, j).start()
            return 0

        lax.fori_loop(0, n_chunk, body, 0)

    def pair_sum(i, j):
        mine = product(i, c, j)
        ps_copy(i, j).wait_recv()
        return mine + got_sib[i, j].astype(jnp.float32)

    for i in range(1, X):
        give_sibling(i)

        def send_chunk(j, _):
            part[i - 1, j] = pair_sum(i, j).astype(jnp.bfloat16)
            p_copy(i, j).start()
            return 0

        lax.fori_loop(0, n_chunk, send_chunk, 0)
    give_sibling(0)
    res_copy.wait()

    def pos_done(i, _):
        pos_copy(i).wait_send()
        return 0

    lax.fori_loop(1, n_ctx, pos_done, 0)

    @pl.when(crossed)
    def _():
        for h in range(heads):
            for j, (src, dst) in enumerate(init_pairs(h)):
                remote(src, dst, init_send.at[h, j], init_recv.at[h, j], partner).wait_send()

            @pl.when(jnp.logical_not(left_out(h)))
            def _():
                o_copy(h, 0).wait_send()

        for j, (src, dst) in enumerate(small_pairs):
            remote(src, dst, small_send.at[j], small_recv.at[j], partner).wait_send()

    @pl.when(helper)
    def _():
        o_copy(max(off, 0), 1).wait_send()

    @pl.when(at_end)
    def _():
        q_copy().wait_send()

    def line_done(idx, _):
        for h in range(heads):

            @pl.when(jnp.logical_not(left_out(h)))
            def _():
                sib_copy(h, idx).wait_send()

            @pl.when((idx <= w) & goes(1, h) & (jnp.logical_not(left_out(h)) | (idx == w)))
            def _():
                line_copy(h, idx, 1).wait_send()

            @pl.when((idx >= w) & goes(0, h) & (jnp.logical_not(left_out(h)) | (idx == w)))
            def _():
                line_copy(h, idx, 0).wait_send()

        return 0

    lax.fori_loop(0, W, line_done, 0)

    def last_chunk(j, _):
        cols = pl.ds(pl.multiple_of(j * CHUNK, CHUNK), CHUNK)
        result = pair_sum(0, j) + res_buf[:, cols].astype(jnp.float32)
        for i in range(1, X):
            p_copy(i, j).wait()
            result = result + got[i - 1, j].astype(jnp.float32)
        for i in range(X):
            ps_copy(i, j).wait_send()
        out_ref[:, cols] = result.astype(out_ref.dtype)
        return 0

    lax.fori_loop(0, n_chunk, last_chunk, 0)


def per_device(n_ctx, n_tp, queries, keys, values, positions, lambda_vecs, head_gain, out_weight, residual):
    rows = queries.shape[0]
    heads, depth = lambda_vecs.shape[1], lambda_vecs.shape[2]
    wide = 2 * depth
    W, X = n_ctx // 2, n_tp // 2
    columns = out_weight.shape[1] // n_tp
    n_chunk = columns // CHUNK
    vmem = pl.BlockSpec(memory_space=pltpu.VMEM)
    hbm = pl.BlockSpec(memory_space=pl.ANY)
    bf16, f32 = jnp.bfloat16, jnp.float32
    dma = pltpu.SemaphoreType.DMA
    return pl.pallas_call(
        functools.partial(layer_kernel, n_ctx, n_tp),
        out_shape=jax.ShapeDtypeStruct((rows, columns), bf16),
        in_specs=[hbm] * 8,
        out_specs=vmem,
        scratch_shapes=[
            pltpu.VMEM((heads + 1, rows, wide), bf16),
            pltpu.VMEM((heads, W, 2, rows, 2 * wide), bf16),
            pltpu.VMEM((n_ctx, 1, rows), jnp.int32),
            pltpu.VMEM((heads, 4, depth), f32),
            pltpu.VMEM((2 * heads, depth), f32),
            pltpu.VMEM((heads, 1, wide), f32),
            pltpu.VMEM((heads, 1, wide), f32),
            pltpu.VMEM((2, rows, 1), jnp.int32),
            pltpu.VMEM((heads + 1, 2, rows, 1), f32),
            pltpu.VMEM((heads + 1, 2, rows, 1), f32),
            pltpu.VMEM((heads + 1, 2, rows, wide), f32),
            pltpu.VMEM((heads + 1, rows, wide), bf16),
            pltpu.VMEM((rows, heads * wide), bf16),
            pltpu.VMEM((n_tp, n_chunk, heads * wide, CHUNK), bf16),
            pltpu.VMEM((rows, columns), bf16),
            pltpu.VMEM((X, n_chunk, rows, CHUNK), bf16),
            pltpu.VMEM((X, n_chunk, rows, CHUNK), bf16),
            pltpu.VMEM((X - 1, n_chunk, rows, CHUNK), bf16),
            pltpu.VMEM((X - 1, n_chunk, rows, CHUNK), bf16),
            dma((heads, 3)),
            dma((heads, 3)),
            dma((2,)),
            dma((2,)),
            dma((n_ctx,)),
            dma((n_ctx,)),
            dma((2, heads, W)),
            dma((heads, W)),
            dma((heads, W)),
            dma((heads, W)),
            dma(()),
            dma(()),
            dma((heads + 1,)),
            dma((heads,)),
            dma((n_tp, n_chunk)),
            dma(()),
            dma((X, n_chunk)),
            dma((X, n_chunk)),
            dma((X - 1, n_chunk)),
            dma((X - 1, n_chunk)),
        ],
        compiler_params=pltpu.CompilerParams(
            collective_id=0, has_side_effects=True, vmem_limit_bytes=56 * 1024 * 1024
        ),
        name="attend_and_project",
    )(
        queries,
        keys,
        values,
        positions.reshape(1, rows),
        jnp.transpose(lambda_vecs, (1, 0, 2)),
        head_gain.reshape(2 * heads, depth),
        out_weight,
        residual,
    )


def solution(mesh):
    placed = (
        P("ctx", "tp"),
        P("ctx", "tp"),
        P("ctx", "tp"),
        P("ctx"),
        P(None, "tp", None),
        P("tp"),
        P("tp", None),
        P("ctx", "tp"),
    )
    return jax.shard_map(
        functools.partial(per_device, mesh.shape["ctx"], mesh.shape["tp"]),
        mesh=mesh,
        in_specs=placed,
        out_specs=P("ctx", "tp"),
        check_vma=False,
    )
```

```python
import functools
import math

import jax
import jax.numpy as jnp
from jax import lax
from jax.experimental import pallas as pl
from jax.experimental.pallas import tpu as pltpu
from jax.sharding import PartitionSpec as P

lambda_init = 0.2
out_factor = 0.8
norm_eps = 1e-05
MASKED = -3e38
LOWEST = -1e30
CHUNK = 256


def layer_kernel(
    n_ctx,
    n_tp,
    q_in,
    k_in,
    v_in,
    pos_in,
    lam_in,
    gain_in,
    w_in,
    res_in,
    out_ref,
    q_buf,
    kv_buf,
    pos_all,
    lam_buf,
    gain_buf,
    lam_wide,
    gain_wide,
    q_pos,
    high,
    total,
    acc,
    stage,
    normed,
    w_buf,
    res_buf,
    part,
    got,
    init_send,
    init_recv,
    small_send,
    small_recv,
    pos_send,
    pos_recv,
    line_send,
    line_recv,
    sib_send,
    sib_recv,
    q_send,
    q_recv,
    o_send,
    o_recv,
    w_local,
    w_send,
    w_recv,
    res_sem,
    p_send,
    p_recv,
):
    heads, rows, wide = stage.shape
    heads -= 1
    depth = wide // 2
    W = n_ctx // 2
    X = n_tp // 2
    n_chunk = w_buf.shape[1]
    off = 0 if W >= 4 else -1
    scale = 1.0 / math.sqrt(depth)
    ctx = lax.axis_index("ctx")
    tp = lax.axis_index("tp")
    w, y = lax.div(ctx, 2), lax.rem(ctx, 2)
    x, c = lax.div(tp, 2), lax.rem(tp, 2)
    crossed = c != y
    straight = c == y
    at_end = (off >= 0) & ((w == 0) | (w == W - 1))
    helper = (off >= 0) & ((w == 1) | (w == W - 2))
    mate = jnp.where(w == 0, 1, jnp.where(w == W - 1, W - 2, jnp.where(w == 1, 0, jnp.where(w == W - 2, W - 1, w))))

    def left_out(h):
        return at_end & (h == off)

    def goes(way, h):
        if way:
            return (w < W - 1) & ((w != W - 2) | (h != off))
        return (w > 0) & ((w != 1) | (h != off))

    def slots(h):
        return 1 + jnp.where(helper & (h == off), 1, 0)

    def dev(a, b):
        return {"ctx": a, "tp": b}

    def remote(src, dst, send, recv, to):
        return pltpu.make_async_remote_copy(
            src_ref=src, dst_ref=dst, send_sem=send, recv_sem=recv, device_id=to, device_id_type=pl.DeviceIdType.MESH
        )

    partner = dev(2 * w + c, 2 * x + y)
    sibling = dev(ctx, 2 * x + 1 - c)
    far = dev(2 * mate + c, 2 * x + y)
    slant = dev(2 * mate + y, 2 * x + 1 - c)

    barrier = pltpu.get_barrier_semaphore()

    def greet(to):
        pl.semaphore_signal(barrier, inc=1, device_id=to, device_id_type=pl.DeviceIdType.MESH)

    greet(sibling)

    @pl.when(crossed)
    def _():
        greet(partner)

    @pl.when(crossed & (at_end | helper))
    def _():
        greet(far)

    @pl.when(at_end | helper)
    def _():
        greet(slant)

    for i in range(1, X):
        greet(dev(ctx, 2 * lax.rem(x + i, X) + c))

    def greet_row(i, _):
        greet(dev(lax.rem(ctx + i, n_ctx), tp))
        return 0

    lax.fori_loop(1, n_ctx, greet_row, 0)
    pl.semaphore_wait(barrier, n_ctx - 1 + 1 + X - 1 + lax.rem(c + y, 2) + jnp.where(at_end | helper, 1 + lax.rem(c + y, 2), 0))

    def init_pairs(h):
        cols = pl.ds(h * wide, wide)
        return (
            (k_in.at[:, cols], kv_buf.at[h, w, y, :, pl.ds(0, wide)]),
            (v_in.at[:, cols], kv_buf.at[h, w, y, :, pl.ds(wide, wide)]),
            (q_in.at[:, cols], q_buf.at[h]),
        )

    small_pairs = ((lam_in, lam_buf), (gain_in, gain_buf))

    @pl.when(straight)
    def _():
        for h in range(heads):
            for j, (src, dst) in enumerate(init_pairs(h)):
                pltpu.make_async_copy(src, dst, init_recv.at[h, j]).start()
            for way in range(2):

                @pl.when(goes(way, h))
                def _():
                    to = dev(ctx + (2 if way else -2), tp)
                    for src, dst in init_pairs(h)[:2]:
                        remote(src, dst, line_send.at[way, h, w], line_recv.at[h, w], to).start()

        for j, (src, dst) in enumerate(small_pairs):
            pltpu.make_async_copy(src, dst, small_recv.at[j]).start()

    @pl.when(crossed)
    def _():
        for h in range(heads):
            for j, (src, dst) in enumerate(init_pairs(h)):
                remote(src, dst, init_send.at[h, j], init_recv.at[h, j], partner).start()
        for j, (src, dst) in enumerate(small_pairs):
            remote(src, dst, small_send.at[j], small_recv.at[j], partner).start()

    def pos_copy(i):
        return remote(
            pos_in,
            pos_all.at[ctx],
            pos_send.at[i],
            pos_recv.at[ctx],
            dev(lax.rem(ctx + i, n_ctx), tp),
        )

    def pos_start(i, _):
        pos_copy(i).start()
        return 0

    pltpu.make_async_copy(pos_in, pos_all.at[ctx], pos_recv.at[ctx]).start()
    lax.fori_loop(1, n_ctx, pos_start, 0)

    col_count = n_chunk * CHUNK
    w_rows = heads * wide

    def w_src(i, j, core):
        start = pl.multiple_of((2 * i + core) * col_count + j * CHUNK, CHUNK)
        return w_in.at[:, pl.ds(start, CHUNK)]

    def w_dst(i, j, group):
        return w_buf.at[i, j, pl.ds(pl.multiple_of(group * w_rows, 16), w_rows)]

    def w_own(i, j):
        return pltpu.make_async_copy(w_src(i, j, c), w_dst(i, j, c), w_local.at[i, j])

    def w_give(i, j):
        return remote(w_src(i, j, 1 - c), w_dst(i, j, c), w_send.at[i, j], w_recv.at[i, j], sibling)

    def w_take(i, j):
        return remote(w_src(i, j, c), w_dst(i, j, 1 - c), w_send.at[i, j], w_recv.at[i, j], sibling)

    w_total = X * n_chunk
    w_per_step = -(-w_total // (W * heads - 1))

    def w_start(k, _):
        i, j = lax.rem(lax.div(k, n_chunk) + x + 1, X), lax.rem(k, n_chunk)
        w_own(i, j).start()
        w_give(i, j).start()
        return 0

    res_copy = pltpu.make_async_copy(res_in, res_buf, res_sem)

    def line_copy(h, idx, way):
        block = kv_buf.at[h, idx, c]
        to = dev(ctx + (2 if way else -2), tp)
        return remote(block, block, line_send.at[way, h, idx], line_recv.at[h, idx], to)

    def sib_copy(h, idx):
        block = kv_buf.at[h, idx, c]
        return remote(block, block, sib_send.at[h, idx], sib_recv.at[h, idx], sibling)

    def sib_wait(h, idx):
        block = kv_buf.at[h, idx, 1 - c]
        remote(block, block, sib_send.at[h, idx], sib_recv.at[h, idx], sibling).wait_recv()

    def q_copy():
        return remote(q_buf.at[max(off, 0)], q_buf.at[heads], q_send, q_recv, dev(2 * mate + y, tp))

    def position_column(row):
        line = pos_all[row]
        square = (rows, rows)
        same = lax.broadcasted_iota(jnp.int32, square, 0) == lax.broadcasted_iota(jnp.int32, square, 1)
        return jnp.sum(jnp.where(same, jnp.broadcast_to(line, square), 0), -1, keepdims=True)

    def attend(h, idx):
        def one(k, _):
            e = h + k * (heads - h)

            @pl.when((k > 0) & (idx == w))
            def _():
                q_copy().wait_recv()

            k_pos = jnp.concatenate([pos_all[2 * idx], pos_all[2 * idx + 1]], axis=1)
            allowed = k_pos <= q_pos[k]
            value = kv_buf[h, idx, :, :, pl.ds(wide, wide)].reshape(2 * rows, wide)
            before = [high[e, a] for a in range(2)]
            sums = [total[e, a] for a in range(2)]
            held = [acc[e, a] for a in range(2)]
            for a in range(2):
                query = q_buf[e, :, pl.ds(a * depth, depth)]
                key = kv_buf[h, idx, :, :, pl.ds(a * depth, depth)].reshape(2 * rows, depth)
                scores = (
                    lax.dot_general(query, key, (((1,), (1,)), ((), ())), preferred_element_type=jnp.float32) * scale
                )
                scores = jnp.where(allowed, scores, MASKED)
                now = jnp.maximum(before[a], jnp.max(scores, -1, keepdims=True))
                keep = jnp.exp(before[a] - now)
                expo = jnp.exp(scores - now)
                before[a] = now
                sums[a] = sums[a] * keep + jnp.sum(expo, -1, keepdims=True)
                held[a] = held[a] * keep + jnp.dot(
                    expo.astype(jnp.bfloat16), value, preferred_element_type=jnp.float32
                )
            for a in range(2):
                high[e, a] = before[a]
                total[e, a] = sums[a]
                acc[e, a] = held[a]
            return 0

        lax.fori_loop(0, slots(h), one, 0)

    def head_columns(g, h):
        return pl.ds(pl.multiple_of((g * heads + h) * wide, wide), wide)

    def o_copy(h, k, core):
        e = h + k * (heads - h)
        to = dev(2 * (w + k * (mate - w)) + c, 2 * x + core)
        return remote(stage.at[e], normed.at[:, head_columns(y, h)], o_send.at[core, e], o_recv.at[y, h], to)

    def o_wait(g, h):
        remote(stage.at[h], normed.at[:, head_columns(g, h)], o_send.at[0, h], o_recv.at[g, h], sibling).wait_recv()

    def finish(h):
        def one(k, _):
            e = h + k * (heads - h)
            first = acc[e, 0] / total[e, 0]
            second = acc[e, 1] / total[e, 1]
            diff = first - lam_wide[h] * second
            mean_square = jnp.mean(diff * diff, -1, keepdims=True)
            result = (out_factor * diff * lax.rsqrt(mean_square + norm_eps) * gain_wide[h]).astype(jnp.bfloat16)

            stage[e] = result

            @pl.when(straight & (k == 0))
            def _():
                normed[:, head_columns(y, h)] = result

            for core in range(2):

                @pl.when(crossed | (k > 0) | (c != core))
                def _():
                    o_copy(h, k, core).start()

            return 0

        lax.fori_loop(0, slots(h), one, 0)

    res_copy.start()

    high[...] = jnp.full(high.shape, LOWEST, jnp.float32)
    total[...] = jnp.zeros(total.shape, jnp.float32)
    acc[...] = jnp.zeros(acc.shape, jnp.float32)

    def step(t, _):
        s, h = lax.div(t, heads), lax.rem(t, heads)

        @pl.when(s == 0)
        def _():
            cols = pl.ds(0, wide)
            src = k_in.at[:, cols]
            pltpu.make_async_copy(src, kv_buf.at[h, w, c, :, cols], init_recv.at[h, 0]).wait()
            pltpu.make_async_copy(src, kv_buf.at[h, w, c, :, pl.ds(wide, wide)], init_recv.at[h, 1]).wait()

            for way in range(2):

                @pl.when(crossed & goes(way, h))
                def _():
                    line_copy(h, w, way).start()

            @pl.when(jnp.logical_not(left_out(h)))
            def _():
                sib_copy(h, w).start()

            pltpu.make_async_copy(src, q_buf.at[h], init_recv.at[h, 2]).wait()

            @pl.when(left_out(h))
            def _():
                q_copy().start()

        @pl.when(t == heads)
        def _():
            for j, (src, dst) in enumerate(small_pairs):
                pltpu.make_async_copy(src, dst, small_recv.at[j]).wait()
            vecs = lam_buf[...]
            lam = (
                jnp.exp(jnp.sum(vecs[:, 0] * vecs[:, 1], -1, keepdims=True))
                - jnp.exp(jnp.sum(vecs[:, 2] * vecs[:, 3], -1, keepdims=True))
                + lambda_init
            )
            for i in range(heads):
                lam_wide[i] = jnp.broadcast_to(lam[i : i + 1], (1, wide))
                gain_wide[i] = jnp.concatenate([gain_buf[pl.ds(2 * i, 1)], gain_buf[pl.ds(2 * i + 1, 1)]], axis=1)

        @pl.when((s > 0) & (s < W) & jnp.logical_not(left_out(h)))
        def _():
            for way, idx in ((1, w - s), (0, w + s)):

                @pl.when((idx >= 0) & (idx < W))
                def _():
                    line_copy(h, idx, way).wait_recv()

                    @pl.when(goes(way, h))
                    def _():
                        line_copy(h, idx, way).start()

                    sib_copy(h, idx).start()

        lax.fori_loop(
            jnp.clip((t - 1) * w_per_step, 0, w_total), jnp.clip(t * w_per_step, 0, w_total), w_start, 0
        )

        @pl.when(t == 1)
        def _():
            def pos_wait(i, _):
                frm = lax.rem(ctx + i, n_ctx)
                remote(pos_in, pos_all.at[frm], pos_send.at[i], pos_recv.at[frm], sibling).wait_recv()
                return 0

            pltpu.make_async_copy(pos_in, pos_all.at[ctx], pos_recv.at[ctx]).wait()
            lax.fori_loop(1, n_ctx, pos_wait, 0)
            q_pos[0] = position_column(2 * w + c)
            q_pos[1] = position_column(2 * mate + c)

        s1, h1 = lax.div(t + heads - 1, heads) - 1, lax.rem(t + heads - 1, heads)

        @pl.when((t > 0) & jnp.logical_not(left_out(h1)))
        def _():
            @pl.when(w - s1 >= 0)
            def _():
                sib_wait(h1, w - s1)
                attend(h1, w - s1)

            @pl.when((s1 > 0) & (w + s1 < W))
            def _():
                sib_wait(h1, w + s1)
                attend(h1, w + s1)

            @pl.when(s1 == jnp.maximum(w, W - 1 - w))
            def _():
                finish(h1)

        return 0

    lax.fori_loop(0, W * heads + 1, step, 0)

    for h in range(heads):
        for g in range(2):

            @pl.when(crossed | (y != g) | left_out(h))
            def _():
                o_wait(g, h)

    def product(i, j):
        w_own(i, j).wait()
        w_take(i, j).wait_recv()
        return jnp.dot(normed[...], w_buf[i, j], preferred_element_type=jnp.float32)

    def p_copy(i, j):
        to = dev(ctx, 2 * lax.rem(x + i, X) + c)
        return remote(part.at[i - 1, j], got.at[i - 1, j], p_send.at[i - 1, j], p_recv.at[i - 1, j], to)

    for i in range(1, X):

        def send_chunk(j, _):
            part[i - 1, j] = product(lax.rem(x + i, X), j).astype(jnp.bfloat16)
            p_copy(i, j).start()
            return 0

        lax.fori_loop(0, n_chunk, send_chunk, 0)
    res_copy.wait()

    def w_done(k, _):
        w_give(lax.div(k, n_chunk), lax.rem(k, n_chunk)).wait_send()
        return 0

    lax.fori_loop(0, w_total, w_done, 0)

    def pos_done(i, _):
        pos_copy(i).wait_send()
        return 0

    lax.fori_loop(1, n_ctx, pos_done, 0)

    @pl.when(crossed)
    def _():
        for h in range(heads):
            for j, (src, dst) in enumerate(init_pairs(h)):
                remote(src, dst, init_send.at[h, j], init_recv.at[h, j], partner).wait_send()

            @pl.when(jnp.logical_not(left_out(h)))
            def _():
                o_copy(h, 0, 1 - c).wait_send()
                o_copy(h, 0, c).wait_send()

        for j, (src, dst) in enumerate(small_pairs):
            remote(src, dst, small_send.at[j], small_recv.at[j], partner).wait_send()

    @pl.when(straight)
    def _():
        for h in range(heads):

            @pl.when(jnp.logical_not(left_out(h)))
            def _():
                o_copy(h, 0, 1 - c).wait_send()

    @pl.when(helper)
    def _():
        for core in range(2):
            o_copy(max(off, 0), 1, core).wait_send()

    @pl.when(at_end)
    def _():
        q_copy().wait_send()

    def line_done(idx, _):
        for h in range(heads):

            @pl.when(jnp.logical_not(left_out(h)))
            def _():
                sib_copy(h, idx).wait_send()

            @pl.when((idx <= w) & goes(1, h) & (jnp.logical_not(left_out(h)) | (idx == w)))
            def _():
                line_copy(h, idx, 1).wait_send()

            @pl.when((idx >= w) & goes(0, h) & (jnp.logical_not(left_out(h)) | (idx == w)))
            def _():
                line_copy(h, idx, 0).wait_send()

        return 0

    lax.fori_loop(0, W, line_done, 0)

    def last_chunk(j, _):
        cols = pl.ds(pl.multiple_of(j * CHUNK, CHUNK), CHUNK)
        result = product(x, j) + res_buf[:, cols].astype(jnp.float32)
        for i in range(1, X):
            p_copy(i, j).wait()
            result = result + got[i - 1, j].astype(jnp.float32)
        out_ref[:, cols] = result.astype(out_ref.dtype)
        return 0

    lax.fori_loop(0, n_chunk, last_chunk, 0)


def per_device(n_ctx, n_tp, queries, keys, values, positions, lambda_vecs, head_gain, out_weight, residual):
    rows = queries.shape[0]
    heads, depth = lambda_vecs.shape[1], lambda_vecs.shape[2]
    wide = 2 * depth
    W, X = n_ctx // 2, n_tp // 2
    columns = out_weight.shape[1] // n_tp
    n_chunk = columns // CHUNK
    vmem = pl.BlockSpec(memory_space=pltpu.VMEM)
    hbm = pl.BlockSpec(memory_space=pl.ANY)
    bf16, f32 = jnp.bfloat16, jnp.float32
    dma = pltpu.SemaphoreType.DMA
    return pl.pallas_call(
        functools.partial(layer_kernel, n_ctx, n_tp),
        out_shape=jax.ShapeDtypeStruct((rows, columns), bf16),
        in_specs=[hbm] * 8,
        out_specs=vmem,
        scratch_shapes=[
            pltpu.VMEM((heads + 1, rows, wide), bf16),
            pltpu.VMEM((heads, W, 2, rows, 2 * wide), bf16),
            pltpu.VMEM((n_ctx, 1, rows), jnp.int32),
            pltpu.VMEM((heads, 4, depth), f32),
            pltpu.VMEM((2 * heads, depth), f32),
            pltpu.VMEM((heads, 1, wide), f32),
            pltpu.VMEM((heads, 1, wide), f32),
            pltpu.VMEM((2, rows, 1), jnp.int32),
            pltpu.VMEM((heads + 1, 2, rows, 1), f32),
            pltpu.VMEM((heads + 1, 2, rows, 1), f32),
            pltpu.VMEM((heads + 1, 2, rows, wide), f32),
            pltpu.VMEM((heads + 1, rows, wide), bf16),
            pltpu.VMEM((rows, 2 * heads * wide), bf16),
            pltpu.VMEM((X, n_chunk, 2 * heads * wide, CHUNK), bf16),
            pltpu.VMEM((rows, columns), bf16),
            pltpu.VMEM((X - 1, n_chunk, rows, CHUNK), bf16),
            pltpu.VMEM((X - 1, n_chunk, rows, CHUNK), bf16),
            dma((heads, 3)),
            dma((heads, 3)),
            dma((2,)),
            dma((2,)),
            dma((n_ctx,)),
            dma((n_ctx,)),
            dma((2, heads, W)),
            dma((heads, W)),
            dma((heads, W)),
            dma((heads, W)),
            dma(()),
            dma(()),
            dma((2, heads + 1)),
            dma((2, heads)),
            dma((X, n_chunk)),
            dma((X, n_chunk)),
            dma((X, n_chunk)),
            dma(()),
            dma((X - 1, n_chunk)),
            dma((X - 1, n_chunk)),
        ],
        compiler_params=pltpu.CompilerParams(
            collective_id=0, has_side_effects=True, vmem_limit_bytes=56 * 1024 * 1024
        ),
        name="attend_and_project",
    )(
        queries,
        keys,
        values,
        positions.reshape(1, rows),
        jnp.transpose(lambda_vecs, (1, 0, 2)),
        head_gain.reshape(2 * heads, depth),
        out_weight,
        residual,
    )


def solution(mesh):
    placed = (
        P("ctx", "tp"),
        P("ctx", "tp"),
        P("ctx", "tp"),
        P("ctx"),
        P(None, "tp", None),
        P("tp"),
        P("tp", None),
        P("ctx", "tp"),
    )
    return jax.shard_map(
        functools.partial(per_device, mesh.shape["ctx"], mesh.shape["tp"]),
        mesh=mesh,
        in_specs=placed,
        out_specs=P("ctx", "tp"),
        check_vma=False,
    )
```

```python
import functools
import math

import jax
import jax.numpy as jnp
from jax import lax
from jax.experimental import pallas as pl
from jax.experimental.pallas import tpu as pltpu
from jax.sharding import PartitionSpec as P

lambda_init = 0.2
out_factor = 0.8
norm_eps = 1e-05
MASKED = -3e38
LOWEST = -1e30
CHUNK = 256


def layer_kernel(
    n_ctx,
    n_tp,
    q_in,
    k_in,
    v_in,
    pos_in,
    lam_in,
    gain_in,
    w_in,
    res_in,
    out_ref,
    q_buf,
    kv_buf,
    pos_all,
    lam_buf,
    gain_buf,
    lam_wide,
    gain_wide,
    q_pos,
    high,
    total,
    acc,
    stage,
    normed,
    w_buf,
    res_buf,
    part_sib,
    got_sib,
    part,
    got,
    init_send,
    init_recv,
    small_send,
    small_recv,
    pos_send,
    pos_recv,
    line_send,
    line_recv,
    sib_send,
    sib_recv,
    q_send,
    q_recv,
    o_send,
    o_recv,
    w_sem,
    res_sem,
    ps_send,
    ps_recv,
    p_send,
    p_recv,
):
    heads, rows, wide = stage.shape
    heads -= 1
    depth = wide // 2
    W = n_ctx // 2
    X = n_tp // 2
    n_chunk = w_buf.shape[1]
    off = heads - 1 if W >= 4 else -1
    scale = math.log2(math.e) / math.sqrt(depth)
    ctx = lax.axis_index("ctx")
    tp = lax.axis_index("tp")
    w, y = lax.div(ctx, 2), lax.rem(ctx, 2)
    x, c = lax.div(tp, 2), lax.rem(tp, 2)
    crossed = c != y
    straight = c == y
    at_end = (off >= 0) & ((w == 0) | (w == W - 1))
    helper = (off >= 0) & ((w == 1) | (w == W - 2))
    mate = jnp.where(w == 0, 1, jnp.where(w == W - 1, W - 2, jnp.where(w == 1, 0, jnp.where(w == W - 2, W - 1, w))))

    def left_out(h):
        return at_end & (h == off)

    def goes(way, h):
        if way:
            return (w < W - 1) & ((w != W - 2) | (h != off))
        return (w > 0) & ((w != 1) | (h != off))

    def slots(h):
        return 1 + jnp.where(helper & (h == off), 1, 0)

    def dev(a, b):
        return {"ctx": a, "tp": b}

    def remote(src, dst, send, recv, to):
        return pltpu.make_async_remote_copy(
            src_ref=src, dst_ref=dst, send_sem=send, recv_sem=recv, device_id=to, device_id_type=pl.DeviceIdType.MESH
        )

    partner = dev(2 * w + c, 2 * x + y)
    sibling = dev(ctx, 2 * x + 1 - c)
    far = dev(2 * mate + c, 2 * x + y)

    barrier = pltpu.get_barrier_semaphore()

    def greet(to):
        pl.semaphore_signal(barrier, inc=1, device_id=to, device_id_type=pl.DeviceIdType.MESH)

    greet(sibling)

    @pl.when(crossed)
    def _():
        greet(partner)

    @pl.when(crossed & (at_end | helper))
    def _():
        greet(far)

    for i in range(1, X):
        greet(dev(ctx, 2 * lax.rem(x + i, X) + c))

    def greet_row(i, _):
        greet(dev(lax.rem(ctx + i, n_ctx), tp))
        return 0

    lax.fori_loop(1, n_ctx, greet_row, 0)
    pl.semaphore_wait(barrier, n_ctx - 1 + 1 + X - 1 + lax.rem(c + y, 2) + jnp.where(crossed & (at_end | helper), 1, 0))

    def init_pairs(h):
        cols = pl.ds(h * wide, wide)
        return (
            (k_in.at[:, cols], kv_buf.at[h, w, y, :, pl.ds(0, wide)]),
            (v_in.at[:, cols], kv_buf.at[h, w, y, :, pl.ds(wide, wide)]),
            (q_in.at[:, cols], q_buf.at[h]),
        )

    small_pairs = ((lam_in, lam_buf), (gain_in, gain_buf))

    @pl.when(straight)
    def _():
        for h in range(heads):
            for j, (src, dst) in enumerate(init_pairs(h)):
                pltpu.make_async_copy(src, dst, init_recv.at[h, j]).start()
            for way in range(2):

                @pl.when(goes(way, h))
                def _():
                    to = dev(ctx + (2 if way else -2), tp)
                    for src, dst in init_pairs(h)[:2]:
                        remote(src, dst, line_send.at[way, h, w], line_recv.at[h, w], to).start()

        for j, (src, dst) in enumerate(small_pairs):
            pltpu.make_async_copy(src, dst, small_recv.at[j]).start()

    @pl.when(crossed)
    def _():
        for h in range(heads):
            for j, (src, dst) in enumerate(init_pairs(h)):
                remote(src, dst, init_send.at[h, j], init_recv.at[h, j], partner).start()
        for j, (src, dst) in enumerate(small_pairs):
            remote(src, dst, small_send.at[j], small_recv.at[j], partner).start()

    def pos_copy(i):
        return remote(
            pos_in,
            pos_all.at[ctx],
            pos_send.at[i],
            pos_recv.at[ctx],
            dev(lax.rem(ctx + i, n_ctx), tp),
        )

    def pos_start(i, _):
        pos_copy(i).start()
        return 0

    pltpu.make_async_copy(pos_in, pos_all.at[ctx], pos_recv.at[ctx]).start()
    lax.fori_loop(1, n_ctx, pos_start, 0)

    def w_copy(i, j):
        start = pl.multiple_of((i * n_chunk + j) * CHUNK, CHUNK)
        return pltpu.make_async_copy(w_in.at[:, pl.ds(start, CHUNK)], w_buf.at[i, j], w_sem.at[i, j])

    w_total = n_tp * n_chunk
    w_per_step = -(-w_total // (W * heads - 1))

    def w_start(k, _):
        i, core = lax.rem(lax.div(k, 2 * n_chunk) + x + 1, X), lax.rem(lax.div(k, n_chunk) + c + 1, 2)
        w_copy(2 * i + core, lax.rem(k, n_chunk)).start()
        return 0

    res_copy = pltpu.make_async_copy(res_in, res_buf, res_sem)

    def line_copy(h, idx, way):
        block = kv_buf.at[h, idx, c]
        to = dev(ctx + (2 if way else -2), tp)
        return remote(block, block, line_send.at[way, h, idx], line_recv.at[h, idx], to)

    def sib_copy(h, idx):
        block = kv_buf.at[h, idx, c]
        return remote(block, block, sib_send.at[h, idx], sib_recv.at[h, idx], sibling)

    def sib_wait(h, idx):
        block = kv_buf.at[h, idx, 1 - c]
        remote(block, block, sib_send.at[h, idx], sib_recv.at[h, idx], sibling).wait_recv()

    def q_copy():
        return remote(q_buf.at[max(off, 0)], q_buf.at[heads], q_send, q_recv, dev(2 * mate + y, tp))

    def position_column(row):
        line = pos_all[row]
        square = (rows, rows)
        same = lax.broadcasted_iota(jnp.int32, square, 0) == lax.broadcasted_iota(jnp.int32, square, 1)
        return jnp.sum(jnp.where(same, jnp.broadcast_to(line, square), 0), -1, keepdims=True)

    def attend(h, blocks):
        def one(k, _):
            e = h + k * (heads - h)
            allowed = [
                jnp.concatenate([pos_all[2 * idx], pos_all[2 * idx + 1]], axis=1) <= q_pos[k] for idx in blocks
            ]
            values = [kv_buf[h, idx, :, :, pl.ds(wide, wide)].reshape(2 * rows, wide) for idx in blocks]
            fresh = []
            for a in range(2):
                query = q_buf[e, :, pl.ds(a * depth, depth)]
                scores = []
                for idx, mask in zip(blocks, allowed):
                    key = kv_buf[h, idx, :, :, pl.ds(a * depth, depth)].reshape(2 * rows, depth)
                    raw = lax.dot_general(
                        query, key, (((1,), (1,)), ((), ())), preferred_element_type=jnp.float32
                    )
                    scores.append(jnp.where(mask, raw, MASKED))
                before = high[e, a]
                now = before
                for part_scores in scores:
                    now = jnp.maximum(now, jnp.max(part_scores, -1, keepdims=True))
                keep = jnp.exp2((before - now) * scale)
                sums = total[e, a] * keep
                held = acc[e, a] * jnp.concatenate([keep] * (wide // 128), axis=1)
                for part_scores, value in zip(scores, values):
                    expo = jnp.exp2((part_scores - now[:, :1]) * scale)
                    sums = sums + jnp.sum(expo, -1, keepdims=True)
                    held = held + jnp.dot(expo.astype(jnp.bfloat16), value, preferred_element_type=jnp.float32)
                fresh.append((now, sums, held))
            for a in range(2):
                high[e, a], total[e, a], acc[e, a] = fresh[a]
            return 0

        lax.fori_loop(0, slots(h), one, 0)

    def head_columns(h):
        return pl.ds(pl.multiple_of(h * wide, wide), wide)

    def o_copy(h, k):
        e = h + k * (heads - h)
        to = dev(2 * (w + k * (mate - w)) + c, 2 * x + y)
        return remote(stage.at[e], normed.at[:, head_columns(h)], o_send.at[e], o_recv.at[h], to)

    def finish(h):
        def one(k, _):
            e = h + k * (heads - h)
            first = acc[e, 0] / total[e, 0, :, :1]
            second = acc[e, 1] / total[e, 1, :, :1]
            diff = first - lam_wide[h] * second
            mean_square = jnp.mean(diff * diff, -1, keepdims=True)
            result = (out_factor * diff * lax.rsqrt(mean_square + norm_eps) * gain_wide[h]).astype(jnp.bfloat16)

            @pl.when(straight & (k == 0))
            def _():
                normed[:, head_columns(h)] = result

            @pl.when(crossed | (k > 0))
            def _():
                stage[e] = result
                o_copy(h, k).start()

            return 0

        lax.fori_loop(0, slots(h), one, 0)

    res_copy.start()

    high[...] = jnp.full(high.shape, LOWEST, jnp.float32)
    total[...] = jnp.zeros(total.shape, jnp.float32)
    acc[...] = jnp.zeros(acc.shape, jnp.float32)

    def step(t, _):
        s, h = lax.div(t, heads), lax.rem(t, heads)

        @pl.when(s == 0)
        def _():
            cols = pl.ds(0, wide)
            src = k_in.at[:, cols]
            pltpu.make_async_copy(src, kv_buf.at[h, w, c, :, cols], init_recv.at[h, 0]).wait()
            pltpu.make_async_copy(src, kv_buf.at[h, w, c, :, pl.ds(wide, wide)], init_recv.at[h, 1]).wait()

            for way in range(2):

                @pl.when(crossed & goes(way, h))
                def _():
                    line_copy(h, w, way).start()

            @pl.when(jnp.logical_not(left_out(h)))
            def _():
                sib_copy(h, w).start()

            pltpu.make_async_copy(src, q_buf.at[h], init_recv.at[h, 2]).wait()

            @pl.when(left_out(h))
            def _():
                q_copy().start()

        @pl.when(t == heads)
        def _():
            for j, (src, dst) in enumerate(small_pairs):
                pltpu.make_async_copy(src, dst, small_recv.at[j]).wait()
            vecs = lam_buf[...]
            lam = (
                jnp.exp(jnp.sum(vecs[:, 0] * vecs[:, 1], -1, keepdims=True))
                - jnp.exp(jnp.sum(vecs[:, 2] * vecs[:, 3], -1, keepdims=True))
                + lambda_init
            )
            for i in range(heads):
                lam_wide[i] = jnp.broadcast_to(lam[i : i + 1], (1, wide))
                gain_wide[i] = jnp.concatenate([gain_buf[pl.ds(2 * i, 1)], gain_buf[pl.ds(2 * i + 1, 1)]], axis=1)

        @pl.when((s > 0) & (s < W) & jnp.logical_not(left_out(h)))
        def _():
            for way, idx in ((1, w - s), (0, w + s)):

                @pl.when((idx >= 0) & (idx < W))
                def _():
                    line_copy(h, idx, way).wait_recv()

                    @pl.when(goes(way, h))
                    def _():
                        line_copy(h, idx, way).start()

                    sib_copy(h, idx).start()

        lax.fori_loop(
            jnp.clip((t - 1) * w_per_step, 0, w_total), jnp.clip(t * w_per_step, 0, w_total), w_start, 0
        )

        @pl.when(t == 1)
        def _():
            def pos_wait(i, _):
                frm = lax.rem(ctx + i, n_ctx)
                remote(pos_in, pos_all.at[frm], pos_send.at[i], pos_recv.at[frm], sibling).wait_recv()
                return 0

            pltpu.make_async_copy(pos_in, pos_all.at[ctx], pos_recv.at[ctx]).wait()
            lax.fori_loop(1, n_ctx, pos_wait, 0)
            q_pos[0] = jnp.broadcast_to(position_column(2 * w + c), q_pos.shape[1:])
            q_pos[1] = jnp.broadcast_to(position_column(2 * mate + c), q_pos.shape[1:])

        s1, h1 = lax.div(t + heads - 1, heads) - 1, lax.rem(t + heads - 1, heads)

        @pl.when((t > 0) & jnp.logical_not(left_out(h1)))
        def _():
            @pl.when(helper & (t == off + 1))
            def _():
                q_copy().wait_recv()

            on_left, on_right = w - s1 >= 0, (s1 > 0) & (w + s1 < W)

            @pl.when(on_left & on_right)
            def _():
                sib_wait(h1, w - s1)
                sib_wait(h1, w + s1)
                attend(h1, (w - s1, w + s1))

            @pl.when(on_left != on_right)
            def _():
                idx = jnp.where(on_left, w - s1, w + s1)
                sib_wait(h1, idx)
                attend(h1, (idx,))

            @pl.when(s1 == jnp.maximum(w, W - 1 - w))
            def _():
                finish(h1)

        return 0

    lax.fori_loop(0, W * heads + 1, step, 0)

    for h in range(heads):

        @pl.when(crossed | left_out(h))
        def _():
            o_copy(h, 0).wait_recv()

    def product(i, core, j):
        target = 2 * lax.rem(x + i, X) + core
        w_copy(target, j).wait()
        return jnp.dot(normed[...], w_buf[target, j], preferred_element_type=jnp.float32)

    def ps_copy(i, j):
        return remote(part_sib.at[i, j], got_sib.at[i, j], ps_send.at[i, j], ps_recv.at[i, j], sibling)

    def p_copy(i, j):
        to = dev(ctx, 2 * lax.rem(x + i, X) + c)
        return remote(part.at[i - 1, j], got.at[i - 1, j], p_send.at[i - 1, j], p_recv.at[i - 1, j], to)

    def give_sibling(i):
        def body(j, _):
            part_sib[i, j] = product(i, 1 - c, j).astype(jnp.bfloat16)
            ps_copy(i, j).start()
            return 0

        lax.fori_loop(0, n_chunk, body, 0)

    def pair_sum(i, j):
        mine = product(i, c, j)
        ps_copy(i, j).wait_recv()
        return mine + got_sib[i, j].astype(jnp.float32)

    for i in range(1, X):

        def send_chunk(j, _):
            @pl.when(j < n_chunk)
            def _():
                part_sib[i, j] = product(i, 1 - c, j).astype(jnp.bfloat16)
                ps_copy(i, j).start()

            @pl.when(j >= 2)
            def _():
                part[i - 1, j - 2] = pair_sum(i, j - 2).astype(jnp.bfloat16)
                p_copy(i, j - 2).start()

            return 0

        lax.fori_loop(0, n_chunk + 2, send_chunk, 0)
    give_sibling(0)
    res_copy.wait()

    def pos_done(i, _):
        pos_copy(i).wait_send()
        return 0

    lax.fori_loop(1, n_ctx, pos_done, 0)

    @pl.when(crossed)
    def _():
        for h in range(heads):
            for j, (src, dst) in enumerate(init_pairs(h)):
                remote(src, dst, init_send.at[h, j], init_recv.at[h, j], partner).wait_send()

            @pl.when(jnp.logical_not(left_out(h)))
            def _():
                o_copy(h, 0).wait_send()

        for j, (src, dst) in enumerate(small_pairs):
            remote(src, dst, small_send.at[j], small_recv.at[j], partner).wait_send()

    @pl.when(helper)
    def _():
        o_copy(max(off, 0), 1).wait_send()

    @pl.when(at_end)
    def _():
        q_copy().wait_send()

    def line_done(idx, _):
        for h in range(heads):

            @pl.when(jnp.logical_not(left_out(h)))
            def _():
                sib_copy(h, idx).wait_send()

            @pl.when((idx <= w) & goes(1, h) & (jnp.logical_not(left_out(h)) | (idx == w)))
            def _():
                line_copy(h, idx, 1).wait_send()

            @pl.when((idx >= w) & goes(0, h) & (jnp.logical_not(left_out(h)) | (idx == w)))
            def _():
                line_copy(h, idx, 0).wait_send()

        return 0

    lax.fori_loop(0, W, line_done, 0)

    def last_chunk(j, _):
        cols = pl.ds(pl.multiple_of(j * CHUNK, CHUNK), CHUNK)
        result = pair_sum(0, j) + res_buf[:, cols].astype(jnp.float32)
        for i in range(1, X):
            p_copy(i, j).wait()
            result = result + got[i - 1, j].astype(jnp.float32)
        for i in range(X):
            ps_copy(i, j).wait_send()
        out_ref[:, cols] = result.astype(out_ref.dtype)
        return 0

    lax.fori_loop(0, n_chunk, last_chunk, 0)


def per_device(n_ctx, n_tp, queries, keys, values, positions, lambda_vecs, head_gain, out_weight, residual):
    rows = queries.shape[0]
    heads, depth = lambda_vecs.shape[1], lambda_vecs.shape[2]
    wide = 2 * depth
    W, X = n_ctx // 2, n_tp // 2
    columns = out_weight.shape[1] // n_tp
    n_chunk = columns // CHUNK
    vmem = pl.BlockSpec(memory_space=pltpu.VMEM)
    hbm = pl.BlockSpec(memory_space=pl.ANY)
    bf16, f32 = jnp.bfloat16, jnp.float32
    dma = pltpu.SemaphoreType.DMA
    return pl.pallas_call(
        functools.partial(layer_kernel, n_ctx, n_tp),
        out_shape=jax.ShapeDtypeStruct((rows, columns), bf16),
        in_specs=[hbm] * 8,
        out_specs=vmem,
        scratch_shapes=[
            pltpu.VMEM((heads + 1, rows, wide), bf16),
            pltpu.VMEM((heads, W, 2, rows, 2 * wide), bf16),
            pltpu.VMEM((n_ctx, 1, rows), jnp.int32),
            pltpu.VMEM((heads, 4, depth), f32),
            pltpu.VMEM((2 * heads, depth), f32),
            pltpu.VMEM((heads, 1, wide), f32),
            pltpu.VMEM((heads, 1, wide), f32),
            pltpu.VMEM((2, rows, 2 * rows), jnp.int32),
            pltpu.VMEM((heads + 1, 2, rows, 128), f32),
            pltpu.VMEM((heads + 1, 2, rows, 128), f32),
            pltpu.VMEM((heads + 1, 2, rows, wide), f32),
            pltpu.VMEM((heads + 1, rows, wide), bf16),
            pltpu.VMEM((rows, heads * wide), bf16),
            pltpu.VMEM((n_tp, n_chunk, heads * wide, CHUNK), bf16),
            pltpu.VMEM((rows, columns), bf16),
            pltpu.VMEM((X, n_chunk, rows, CHUNK), bf16),
            pltpu.VMEM((X, n_chunk, rows, CHUNK), bf16),
            pltpu.VMEM((X - 1, n_chunk, rows, CHUNK), bf16),
            pltpu.VMEM((X - 1, n_chunk, rows, CHUNK), bf16),
            dma((heads, 3)),
            dma((heads, 3)),
            dma((2,)),
            dma((2,)),
            dma((n_ctx,)),
            dma((n_ctx,)),
            dma((2, heads, W)),
            dma((heads, W)),
            dma((heads, W)),
            dma((heads, W)),
            dma(()),
            dma(()),
            dma((heads + 1,)),
            dma((heads,)),
            dma((n_tp, n_chunk)),
            dma(()),
            dma((X, n_chunk)),
            dma((X, n_chunk)),
            dma((X - 1, n_chunk)),
            dma((X - 1, n_chunk)),
        ],
        compiler_params=pltpu.CompilerParams(
            collective_id=0, has_side_effects=True, vmem_limit_bytes=56 * 1024 * 1024
        ),
        name="attend_and_project",
    )(
        queries,
        keys,
        values,
        positions.reshape(1, rows),
        jnp.transpose(lambda_vecs, (1, 0, 2)),
        head_gain.reshape(2 * heads, depth),
        out_weight,
        residual,
    )


def solution(mesh):
    placed = (
        P("ctx", "tp"),
        P("ctx", "tp"),
        P("ctx", "tp"),
        P("ctx"),
        P(None, "tp", None),
        P("tp"),
        P("tp", None),
        P("ctx", "tp"),
    )
    return jax.shard_map(
        functools.partial(per_device, mesh.shape["ctx"], mesh.shape["tp"]),
        mesh=mesh,
        in_specs=placed,
        out_specs=P("ctx", "tp"),
        check_vma=False,
    )
```

```python
import functools
import math

import jax
import jax.numpy as jnp
from jax import lax
from jax.experimental import pallas as pl
from jax.experimental.pallas import tpu as pltpu
from jax.sharding import PartitionSpec as P

lambda_init = 0.2
out_factor = 0.8
norm_eps = 1e-05
MASKED = -3e38
LOWEST = -1e30
CHUNK = 256


def layer_kernel(
    n_ctx,
    n_tp,
    q_in,
    k_in,
    v_in,
    pos_in,
    lam_in,
    gain_in,
    w_in,
    res_in,
    out_ref,
    q_buf,
    kv_buf,
    pos_all,
    lam_buf,
    gain_buf,
    lam_wide,
    gain_wide,
    q_pos,
    high,
    total,
    acc,
    stage,
    normed,
    w_buf,
    w_sib,
    res_buf,
    part_sib,
    got_sib,
    part,
    got,
    init_send,
    init_recv,
    small_send,
    small_recv,
    pos_send,
    pos_recv,
    line_send,
    line_recv,
    sib_send,
    sib_recv,
    q_send,
    q_recv,
    o_send,
    o_recv,
    w_sem,
    ws_send,
    ws_recv,
    res_sem,
    ps_send,
    ps_recv,
    p_send,
    p_recv,
):
    heads, rows, wide = stage.shape
    heads -= 1
    depth = wide // 2
    W = n_ctx // 2
    X = n_tp // 2
    n_chunk = w_buf.shape[1]
    off = heads - 1 if W >= 4 else -1
    scale = math.log2(math.e) / math.sqrt(depth)
    ctx = lax.axis_index("ctx")
    tp = lax.axis_index("tp")
    w, y = lax.div(ctx, 2), lax.rem(ctx, 2)
    x, c = lax.div(tp, 2), lax.rem(tp, 2)
    crossed = c != y
    straight = c == y
    at_end = (off >= 0) & ((w == 0) | (w == W - 1))
    helper = (off >= 0) & ((w == 1) | (w == W - 2))
    mate = jnp.where(w == 0, 1, jnp.where(w == W - 1, W - 2, jnp.where(w == 1, 0, jnp.where(w == W - 2, W - 1, w))))

    def left_out(h):
        return at_end & (h == off)

    def goes(way, h):
        if way:
            return (w < W - 1) & ((w != W - 2) | (h != off))
        return (w > 0) & ((w != 1) | (h != off))

    def slots(h):
        return 1 + jnp.where(helper & (h == off), 1, 0)

    def dev(a, b):
        return {"ctx": a, "tp": b}

    def remote(src, dst, send, recv, to):
        return pltpu.make_async_remote_copy(
            src_ref=src, dst_ref=dst, send_sem=send, recv_sem=recv, device_id=to, device_id_type=pl.DeviceIdType.MESH
        )

    partner = dev(2 * w + c, 2 * x + y)
    sibling = dev(ctx, 2 * x + 1 - c)
    far = dev(2 * mate + c, 2 * x + y)
    slant = dev(2 * mate + y, 2 * x + 1 - c)

    barrier = pltpu.get_barrier_semaphore()

    def greet(to):
        pl.semaphore_signal(barrier, inc=1, device_id=to, device_id_type=pl.DeviceIdType.MESH)

    greet(sibling)

    @pl.when(crossed)
    def _():
        greet(partner)

    @pl.when(crossed & (at_end | helper))
    def _():
        greet(far)

    @pl.when(at_end | helper)
    def _():
        greet(slant)

    for i in range(1, X):
        greet(dev(ctx, 2 * lax.rem(x + i, X) + c))

    def greet_row(i, _):
        greet(dev(lax.rem(ctx + i, n_ctx), tp))
        return 0

    lax.fori_loop(1, n_ctx, greet_row, 0)
    pl.semaphore_wait(barrier, n_ctx - 1 + 1 + X - 1 + lax.rem(c + y, 2) + jnp.where(at_end | helper, 1 + lax.rem(c + y, 2), 0))

    def init_pairs(h):
        cols = pl.ds(h * wide, wide)
        return (
            (k_in.at[:, cols], kv_buf.at[h, w, y, :, pl.ds(0, wide)]),
            (v_in.at[:, cols], kv_buf.at[h, w, y, :, pl.ds(wide, wide)]),
            (q_in.at[:, cols], q_buf.at[h]),
        )

    small_pairs = ((lam_in, lam_buf), (gain_in, gain_buf))

    @pl.when(straight)
    def _():
        for h in range(heads):
            for j, (src, dst) in enumerate(init_pairs(h)):
                pltpu.make_async_copy(src, dst, init_recv.at[h, j]).start()
            for way in range(2):

                @pl.when(goes(way, h))
                def _():
                    to = dev(ctx + (2 if way else -2), tp)
                    for src, dst in init_pairs(h)[:2]:
                        remote(src, dst, line_send.at[way, h, w], line_recv.at[h, w], to).start()

        for j, (src, dst) in enumerate(small_pairs):
            pltpu.make_async_copy(src, dst, small_recv.at[j]).start()

    @pl.when(crossed)
    def _():
        for h in range(heads):
            for j, (src, dst) in enumerate(init_pairs(h)):
                remote(src, dst, init_send.at[h, j], init_recv.at[h, j], partner).start()
        for j, (src, dst) in enumerate(small_pairs):
            remote(src, dst, small_send.at[j], small_recv.at[j], partner).start()

    def pos_copy(i):
        return remote(
            pos_in,
            pos_all.at[ctx],
            pos_send.at[i],
            pos_recv.at[ctx],
            dev(lax.rem(ctx + i, n_ctx), tp),
        )

    def pos_start(i, _):
        pos_copy(i).start()
        return 0

    pltpu.make_async_copy(pos_in, pos_all.at[ctx], pos_recv.at[ctx]).start()
    lax.fori_loop(1, n_ctx, pos_start, 0)

    def w_copy(i, j):
        start = pl.multiple_of((i * n_chunk + j) * CHUNK, CHUNK)
        return pltpu.make_async_copy(w_in.at[:, pl.ds(start, CHUNK)], w_buf.at[i, j], w_sem.at[i, j])

    w_total = (X + 1) * n_chunk
    w_per_step = -(-w_total // (W * heads - 1))

    def w_start(k, _):
        m = lax.div(k, n_chunk)
        i, core = jnp.where(m < X - 1, m + 1, 0), jnp.where(m == X - 1, 1 - c, c)
        w_copy(2 * lax.rem(x + i, X) + core, lax.rem(k, n_chunk)).start()
        return 0

    ws_total = (X - 1) * n_chunk
    ws_per_step = -(-ws_total // (W * heads - 2))

    def ws_copy(i, j, core):
        start = pl.multiple_of(((2 * lax.rem(x + i + 1, X) + core) * n_chunk + j) * CHUNK, CHUNK)
        return remote(w_in.at[:, pl.ds(start, CHUNK)], w_sib.at[i, j], ws_send.at[i, j], ws_recv.at[i, j], sibling)

    def ws_start(k, _):
        ws_copy(lax.div(k, n_chunk), lax.rem(k, n_chunk), 1 - c).start()
        return 0

    res_copy = pltpu.make_async_copy(res_in, res_buf, res_sem)

    def line_copy(h, idx, way):
        block = kv_buf.at[h, idx, c]
        to = dev(ctx + (2 if way else -2), tp)
        return remote(block, block, line_send.at[way, h, idx], line_recv.at[h, idx], to)

    def sib_copy(h, idx):
        block = kv_buf.at[h, idx, c]
        return remote(block, block, sib_send.at[h, idx], sib_recv.at[h, idx], sibling)

    def sib_wait(h, idx):
        block = kv_buf.at[h, idx, 1 - c]
        remote(block, block, sib_send.at[h, idx], sib_recv.at[h, idx], sibling).wait_recv()

    def q_copy():
        return remote(q_buf.at[max(off, 0)], q_buf.at[heads], q_send, q_recv, dev(2 * mate + y, tp))

    def position_column(row):
        line = pos_all[row]
        square = (rows, rows)
        same = lax.broadcasted_iota(jnp.int32, square, 0) == lax.broadcasted_iota(jnp.int32, square, 1)
        return jnp.sum(jnp.where(same, jnp.broadcast_to(line, square), 0), -1, keepdims=True)

    def attend(h, blocks, last):
        def one(turn, _):
            k = slots(h) - 1 - turn
            e = h + k * (heads - h)
            allowed = [
                jnp.concatenate([pos_all[2 * idx], pos_all[2 * idx + 1]], axis=1) <= q_pos[k] for idx in blocks
            ]
            values = [kv_buf[h, idx, :, :, pl.ds(wide, wide)].reshape(2 * rows, wide) for idx in blocks]
            fresh = []
            for a in range(2):
                query = q_buf[e, :, pl.ds(a * depth, depth)]
                scores = []
                for idx, mask in zip(blocks, allowed):
                    key = kv_buf[h, idx, :, :, pl.ds(a * depth, depth)].reshape(2 * rows, depth)
                    raw = lax.dot_general(
                        query, key, (((1,), (1,)), ((), ())), preferred_element_type=jnp.float32
                    )
                    scores.append(jnp.where(mask, raw, MASKED))
                before = high[e, a]
                now = before
                for part_scores in scores:
                    now = jnp.maximum(now, jnp.max(part_scores, -1, keepdims=True))
                keep = jnp.exp2((before - now) * scale)
                sums = total[e, a] * keep
                held = acc[e, a] * jnp.concatenate([keep] * (wide // 128), axis=1)
                for part_scores, value in zip(scores, values):
                    expo = jnp.exp2((part_scores - now[:, :1]) * scale)
                    sums = sums + jnp.sum(expo, -1, keepdims=True)
                    held = held + jnp.dot(expo.astype(jnp.bfloat16), value, preferred_element_type=jnp.float32)
                fresh.append((now, sums, held))
            for a in range(2):
                high[e, a], total[e, a], acc[e, a] = fresh[a]

            @pl.when(last)
            def _():
                finish(h, k)

            return 0

        lax.fori_loop(0, slots(h), one, 0)

    def head_columns(h):
        return pl.ds(pl.multiple_of(h * wide, wide), wide)

    def o_copy(h, k, core):
        e = h + k * (heads - h)
        to = dev(2 * (w + k * (mate - w)) + c, 2 * x + core)
        return remote(stage.at[e], normed.at[y, :, head_columns(h)], o_send.at[core, e], o_recv.at[y, h], to)

    def o_wait(g, h):
        remote(stage.at[h], normed.at[g, :, head_columns(h)], o_send.at[0, h], o_recv.at[g, h], sibling).wait_recv()

    def finish(h, k):
        e = h + k * (heads - h)
        first = acc[e, 0] / total[e, 0, :, :1]
        second = acc[e, 1] / total[e, 1, :, :1]
        diff = first - lam_wide[h] * second
        mean_square = jnp.mean(diff * diff, -1, keepdims=True)
        result = (out_factor * diff * lax.rsqrt(mean_square + norm_eps) * gain_wide[h]).astype(jnp.bfloat16)
        stage[e] = result

        @pl.when(straight & (k == 0))
        def _():
            normed[y, :, head_columns(h)] = result

        for core in range(2):

            @pl.when(crossed | (k > 0) | (c != core))
            def _():
                o_copy(h, k, core).start()

    res_copy.start()

    high[...] = jnp.full(high.shape, LOWEST, jnp.float32)
    total[...] = jnp.zeros(total.shape, jnp.float32)
    acc[...] = jnp.zeros(acc.shape, jnp.float32)

    def step(t, _):
        s, h = lax.div(t, heads), lax.rem(t, heads)

        @pl.when(s == 0)
        def _():
            cols = pl.ds(0, wide)
            src = k_in.at[:, cols]
            pltpu.make_async_copy(src, kv_buf.at[h, w, c, :, cols], init_recv.at[h, 0]).wait()
            pltpu.make_async_copy(src, kv_buf.at[h, w, c, :, pl.ds(wide, wide)], init_recv.at[h, 1]).wait()

            for way in range(2):

                @pl.when(crossed & goes(way, h))
                def _():
                    line_copy(h, w, way).start()

            @pl.when(jnp.logical_not(left_out(h)))
            def _():
                sib_copy(h, w).start()

            pltpu.make_async_copy(src, q_buf.at[h], init_recv.at[h, 2]).wait()

            @pl.when(left_out(h))
            def _():
                q_copy().start()

        @pl.when(t == heads)
        def _():
            for j, (src, dst) in enumerate(small_pairs):
                pltpu.make_async_copy(src, dst, small_recv.at[j]).wait()
            vecs = lam_buf[...]
            lam = (
                jnp.exp(jnp.sum(vecs[:, 0] * vecs[:, 1], -1, keepdims=True))
                - jnp.exp(jnp.sum(vecs[:, 2] * vecs[:, 3], -1, keepdims=True))
                + lambda_init
            )
            for i in range(heads):
                lam_wide[i] = jnp.broadcast_to(lam[i : i + 1], (1, wide))
                gain_wide[i] = jnp.concatenate([gain_buf[pl.ds(2 * i, 1)], gain_buf[pl.ds(2 * i + 1, 1)]], axis=1)

        @pl.when((s > 0) & (s < W) & jnp.logical_not(left_out(h)))
        def _():
            for way, idx in ((1, w - s), (0, w + s)):

                @pl.when((idx >= 0) & (idx < W))
                def _():
                    line_copy(h, idx, way).wait_recv()

                    @pl.when(goes(way, h))
                    def _():
                        line_copy(h, idx, way).start()

                    sib_copy(h, idx).start()

        lax.fori_loop(
            jnp.clip((t - 1) * w_per_step, 0, w_total), jnp.clip(t * w_per_step, 0, w_total), w_start, 0
        )

        lax.fori_loop(
            jnp.clip((t - 1) * ws_per_step, 0, ws_total), jnp.clip(t * ws_per_step, 0, ws_total), ws_start, 0
        )

        @pl.when(t == 1)
        def _():
            def pos_wait(i, _):
                frm = lax.rem(ctx + i, n_ctx)
                remote(pos_in, pos_all.at[frm], pos_send.at[i], pos_recv.at[frm], sibling).wait_recv()
                return 0

            pltpu.make_async_copy(pos_in, pos_all.at[ctx], pos_recv.at[ctx]).wait()
            lax.fori_loop(1, n_ctx, pos_wait, 0)
            q_pos[0] = jnp.broadcast_to(position_column(2 * w + c), q_pos.shape[1:])
            q_pos[1] = jnp.broadcast_to(position_column(2 * mate + c), q_pos.shape[1:])

        s1, h1 = lax.div(t + heads - 1, heads) - 1, lax.rem(t + heads - 1, heads)

        @pl.when((t > 0) & jnp.logical_not(left_out(h1)))
        def _():
            @pl.when(helper & (t == off + 1))
            def _():
                q_copy().wait_recv()

            last = s1 == jnp.maximum(w, W - 1 - w)
            on_left, on_right = w - s1 >= 0, (s1 > 0) & (w + s1 < W)

            @pl.when(on_left & on_right)
            def _():
                sib_wait(h1, w - s1)
                sib_wait(h1, w + s1)
                attend(h1, (w - s1, w + s1), last)

            @pl.when(on_left != on_right)
            def _():
                idx = jnp.where(on_left, w - s1, w + s1)
                sib_wait(h1, idx)
                attend(h1, (idx,), last)

        return 0

    lax.fori_loop(0, W * heads + 1, step, 0)

    for h in range(heads):
        for g in range(2):

            @pl.when(crossed | (y != g) | left_out(h))
            def _():
                o_wait(g, h)

    def product(i, core, j):
        target = 2 * lax.rem(x + i, X) + core
        w_copy(target, j).wait()
        return jnp.dot(normed[c], w_buf[target, j], preferred_element_type=jnp.float32)

    def ps_copy(j):
        return remote(part_sib.at[j], got_sib.at[j], ps_send.at[j], ps_recv.at[j], sibling)

    def p_copy(i, j):
        to = dev(ctx, 2 * lax.rem(x + i, X) + c)
        return remote(part.at[i - 1, j], got.at[i - 1, j], p_send.at[i - 1, j], p_recv.at[i - 1, j], to)

    for i in range(1, X):

        def send_chunk(j, _):
            ws_copy(i - 1, j, c).wait_recv()
            both = product(i, c, j) + jnp.dot(normed[1 - c], w_sib[i - 1, j], preferred_element_type=jnp.float32)
            part[i - 1, j] = both.astype(jnp.bfloat16)
            p_copy(i, j).start()
            return 0

        lax.fori_loop(0, n_chunk, send_chunk, 0)

    def give_sibling(j, _):
        part_sib[j] = product(0, 1 - c, j).astype(jnp.bfloat16)
        ps_copy(j).start()
        return 0

    lax.fori_loop(0, n_chunk, give_sibling, 0)
    res_copy.wait()

    def ws_done(k, _):
        ws_copy(lax.div(k, n_chunk), lax.rem(k, n_chunk), 1 - c).wait_send()
        return 0

    lax.fori_loop(0, ws_total, ws_done, 0)

    def pos_done(i, _):
        pos_copy(i).wait_send()
        return 0

    lax.fori_loop(1, n_ctx, pos_done, 0)

    @pl.when(crossed)
    def _():
        for h in range(heads):
            for j, (src, dst) in enumerate(init_pairs(h)):
                remote(src, dst, init_send.at[h, j], init_recv.at[h, j], partner).wait_send()

            @pl.when(jnp.logical_not(left_out(h)))
            def _():
                o_copy(h, 0, 1 - c).wait_send()
                o_copy(h, 0, c).wait_send()

        for j, (src, dst) in enumerate(small_pairs):
            remote(src, dst, small_send.at[j], small_recv.at[j], partner).wait_send()

    @pl.when(straight)
    def _():
        for h in range(heads):

            @pl.when(jnp.logical_not(left_out(h)))
            def _():
                o_copy(h, 0, 1 - c).wait_send()

    @pl.when(helper)
    def _():
        for core in range(2):
            o_copy(max(off, 0), 1, core).wait_send()

    @pl.when(at_end)
    def _():
        q_copy().wait_send()

    def line_done(idx, _):
        for h in range(heads):

            @pl.when(jnp.logical_not(left_out(h)))
            def _():
                sib_copy(h, idx).wait_send()

            @pl.when((idx <= w) & goes(1, h) & (jnp.logical_not(left_out(h)) | (idx == w)))
            def _():
                line_copy(h, idx, 1).wait_send()

            @pl.when((idx >= w) & goes(0, h) & (jnp.logical_not(left_out(h)) | (idx == w)))
            def _():
                line_copy(h, idx, 0).wait_send()

        return 0

    lax.fori_loop(0, W, line_done, 0)

    def last_chunk(j, _):
        cols = pl.ds(pl.multiple_of(j * CHUNK, CHUNK), CHUNK)
        mine = product(0, c, j) + res_buf[:, cols].astype(jnp.float32)
        ps_copy(j).wait()
        result = mine + got_sib[j].astype(jnp.float32)
        for i in range(1, X):
            p_copy(i, j).wait()
            result = result + got[i - 1, j].astype(jnp.float32)
        out_ref[:, cols] = result.astype(out_ref.dtype)
        return 0

    lax.fori_loop(0, n_chunk, last_chunk, 0)


def per_device(n_ctx, n_tp, queries, keys, values, positions, lambda_vecs, head_gain, out_weight, residual):
    rows = queries.shape[0]
    heads, depth = lambda_vecs.shape[1], lambda_vecs.shape[2]
    wide = 2 * depth
    W, X = n_ctx // 2, n_tp // 2
    columns = out_weight.shape[1] // n_tp
    n_chunk = columns // CHUNK
    vmem = pl.BlockSpec(memory_space=pltpu.VMEM)
    hbm = pl.BlockSpec(memory_space=pl.ANY)
    bf16, f32 = jnp.bfloat16, jnp.float32
    dma = pltpu.SemaphoreType.DMA
    return pl.pallas_call(
        functools.partial(layer_kernel, n_ctx, n_tp),
        out_shape=jax.ShapeDtypeStruct((rows, columns), bf16),
        in_specs=[hbm] * 8,
        out_specs=vmem,
        scratch_shapes=[
            pltpu.VMEM((heads + 1, rows, wide), bf16),
            pltpu.VMEM((heads, W, 2, rows, 2 * wide), bf16),
            pltpu.VMEM((n_ctx, 1, rows), jnp.int32),
            pltpu.VMEM((heads, 4, depth), f32),
            pltpu.VMEM((2 * heads, depth), f32),
            pltpu.VMEM((heads, 1, wide), f32),
            pltpu.VMEM((heads, 1, wide), f32),
            pltpu.VMEM((2, rows, 2 * rows), jnp.int32),
            pltpu.VMEM((heads + 1, 2, rows, 128), f32),
            pltpu.VMEM((heads + 1, 2, rows, 128), f32),
            pltpu.VMEM((heads + 1, 2, rows, wide), f32),
            pltpu.VMEM((heads + 1, rows, wide), bf16),
            pltpu.VMEM((2, rows, heads * wide), bf16),
            pltpu.VMEM((n_tp, n_chunk, heads * wide, CHUNK), bf16),
            pltpu.VMEM((X - 1, n_chunk, heads * wide, CHUNK), bf16),
            pltpu.VMEM((rows, columns), bf16),
            pltpu.VMEM((n_chunk, rows, CHUNK), bf16),
            pltpu.VMEM((n_chunk, rows, CHUNK), bf16),
            pltpu.VMEM((X - 1, n_chunk, rows, CHUNK), bf16),
            pltpu.VMEM((X - 1, n_chunk, rows, CHUNK), bf16),
            dma((heads, 3)),
            dma((heads, 3)),
            dma((2,)),
            dma((2,)),
            dma((n_ctx,)),
            dma((n_ctx,)),
            dma((2, heads, W)),
            dma((heads, W)),
            dma((heads, W)),
            dma((heads, W)),
            dma(()),
            dma(()),
            dma((2, heads + 1)),
            dma((2, heads)),
            dma((n_tp, n_chunk)),
            dma((X - 1, n_chunk)),
            dma((X - 1, n_chunk)),
            dma(()),
            dma((n_chunk,)),
            dma((n_chunk,)),
            dma((X - 1, n_chunk)),
            dma((X - 1, n_chunk)),
        ],
        compiler_params=pltpu.CompilerParams(
            collective_id=0, has_side_effects=True, vmem_limit_bytes=56 * 1024 * 1024
        ),
        name="attend_and_project",
    )(
        queries,
        keys,
        values,
        positions.reshape(1, rows),
        jnp.transpose(lambda_vecs, (1, 0, 2)),
        head_gain.reshape(2 * heads, depth),
        out_weight,
        residual,
    )


def solution(mesh):
    placed = (
        P("ctx", "tp"),
        P("ctx", "tp"),
        P("ctx", "tp"),
        P("ctx"),
        P(None, "tp", None),
        P("tp"),
        P("tp", None),
        P("ctx", "tp"),
    )
    return jax.shard_map(
        functools.partial(per_device, mesh.shape["ctx"], mesh.shape["tp"]),
        mesh=mesh,
        in_specs=placed,
        out_specs=P("ctx", "tp"),
        check_vma=False,
    )
```

```python
import functools
import math

import jax
import jax.numpy as jnp
from jax import lax
from jax.experimental import pallas as pl
from jax.experimental.pallas import tpu as pltpu
from jax.sharding import PartitionSpec as P

lambda_init = 0.2
out_factor = 0.8
norm_eps = 1e-05
MASKED = -3e38
LOWEST = -1e30
CHUNK = 256


def layer_kernel(
    n_ctx,
    n_tp,
    q_in,
    k_in,
    v_in,
    pos_in,
    lam_in,
    gain_in,
    w_in,
    res_in,
    out_ref,
    q_buf,
    kv_buf,
    pos_all,
    lam_buf,
    gain_buf,
    lam_wide,
    gain_wide,
    q_pos,
    high,
    total,
    acc,
    stage,
    normed,
    w_buf,
    res_buf,
    part_sib,
    got_sib,
    part,
    got,
    init_send,
    init_recv,
    small_send,
    small_recv,
    pos_send,
    pos_recv,
    line_send,
    line_recv,
    sib_send,
    sib_recv,
    q_send,
    q_recv,
    o_send,
    o_recv,
    w_sem,
    res_sem,
    ps_send,
    ps_recv,
    p_send,
    p_recv,
):
    heads, rows, wide = stage.shape
    heads -= 1
    depth = wide // 2
    W = n_ctx // 2
    X = n_tp // 2
    n_chunk = w_buf.shape[1]
    off = heads - 1 if W >= 4 else -1
    scale = math.log2(math.e) / math.sqrt(depth)
    ctx = lax.axis_index("ctx")
    tp = lax.axis_index("tp")
    w, y = lax.div(ctx, 2), lax.rem(ctx, 2)
    x, c = lax.div(tp, 2), lax.rem(tp, 2)
    crossed = c != y
    straight = c == y
    at_end = (off >= 0) & ((w == 0) | (w == W - 1))
    helper = (off >= 0) & ((w == 1) | (w == W - 2))
    mate = jnp.where(w == 0, 1, jnp.where(w == W - 1, W - 2, jnp.where(w == 1, 0, jnp.where(w == W - 2, W - 1, w))))

    def left_out(h):
        return at_end & (h == off)

    def goes(way, h):
        if way:
            return (w < W - 1) & ((w != W - 2) | (h != off))
        return (w > 0) & ((w != 1) | (h != off))

    def slots(h):
        return 1 + jnp.where(helper & (h == off), 1, 0)

    def dev(a, b):
        return {"ctx": a, "tp": b}

    def remote(src, dst, send, recv, to):
        return pltpu.make_async_remote_copy(
            src_ref=src, dst_ref=dst, send_sem=send, recv_sem=recv, device_id=to, device_id_type=pl.DeviceIdType.MESH
        )

    partner = dev(2 * w + c, 2 * x + y)
    sibling = dev(ctx, 2 * x + 1 - c)
    far = dev(2 * mate + c, 2 * x + y)

    barrier = pltpu.get_barrier_semaphore()

    def greet(to):
        pl.semaphore_signal(barrier, inc=1, device_id=to, device_id_type=pl.DeviceIdType.MESH)

    greet(sibling)

    @pl.when(crossed)
    def _():
        greet(partner)

    @pl.when(crossed & (at_end | helper))
    def _():
        greet(far)

    for i in range(1, X):
        greet(dev(ctx, 2 * lax.rem(x + i, X) + c))

    def greet_row(i, _):
        greet(dev(lax.rem(ctx + i, n_ctx), tp))
        return 0

    lax.fori_loop(1, n_ctx, greet_row, 0)
    pl.semaphore_wait(barrier, n_ctx - 1 + 1 + X - 1 + lax.rem(c + y, 2) + jnp.where(crossed & (at_end | helper), 1, 0))

    def init_pairs(h):
        cols = pl.ds(h * wide, wide)
        return (
            (k_in.at[:, cols], kv_buf.at[h, w, y, :, pl.ds(0, wide)]),
            (v_in.at[:, cols], kv_buf.at[h, w, y, :, pl.ds(wide, wide)]),
            (q_in.at[:, cols], q_buf.at[h]),
        )

    small_pairs = ((lam_in, lam_buf), (gain_in, gain_buf))

    def init_start(h):
        @pl.when(straight)
        def _():
            for j, (src, dst) in enumerate(init_pairs(h)):
                pltpu.make_async_copy(src, dst, init_recv.at[h, j]).start()

        @pl.when(crossed)
        def _():
            for j, (src, dst) in enumerate(init_pairs(h)):
                remote(src, dst, init_send.at[h, j], init_recv.at[h, j], partner).start()

    for h in range(min(2, heads)):
        init_start(h)

    @pl.when(straight)
    def _():
        for j, (src, dst) in enumerate(small_pairs):
            pltpu.make_async_copy(src, dst, small_recv.at[j]).start()

    @pl.when(crossed)
    def _():
        for j, (src, dst) in enumerate(small_pairs):
            remote(src, dst, small_send.at[j], small_recv.at[j], partner).start()

    def pos_copy(i):
        return remote(
            pos_in,
            pos_all.at[ctx],
            pos_send.at[i],
            pos_recv.at[ctx],
            dev(lax.rem(ctx + i, n_ctx), tp),
        )

    def pos_start(i, _):
        pos_copy(i).start()
        return 0

    pltpu.make_async_copy(pos_in, pos_all.at[ctx], pos_recv.at[ctx]).start()
    lax.fori_loop(1, n_ctx, pos_start, 0)

    def w_copy(i, j):
        start = pl.multiple_of((i * n_chunk + j) * CHUNK, CHUNK)
        return pltpu.make_async_copy(w_in.at[:, pl.ds(start, CHUNK)], w_buf.at[i, j], w_sem.at[i, j])

    w_total = n_tp * n_chunk
    w_per_step = -(-w_total // (W * heads - 1))

    def w_start(k, _):
        i, core = lax.rem(lax.div(k, 2 * n_chunk) + x + 1, X), lax.rem(lax.div(k, n_chunk) + c + 1, 2)
        w_copy(2 * i + core, lax.rem(k, n_chunk)).start()
        return 0

    res_copy = pltpu.make_async_copy(res_in, res_buf, res_sem)

    def line_copy(h, idx, way):
        block = kv_buf.at[h, idx, c]
        to = dev(ctx + (2 if way else -2), tp)
        return remote(block, block, line_send.at[way, h, idx], line_recv.at[h, idx], to)

    def piece(way, t):
        s, h = lax.div(t + heads, heads) - 1, lax.rem(t + heads, heads)
        idx = w - s if way else w + s
        return h, idx, (s >= 0) & (idx >= 0) & (idx < W) & goes(way, h)

    def pace(way, t):
        h, idx, there = piece(way, t - 2)

        @pl.when(there)
        def _():
            line_copy(h, idx, way).wait_send()

    def sib_copy(h, idx):
        block = kv_buf.at[h, idx, c]
        return remote(block, block, sib_send.at[h, idx], sib_recv.at[h, idx], sibling)

    def sib_wait(h, idx):
        block = kv_buf.at[h, idx, 1 - c]
        remote(block, block, sib_send.at[h, idx], sib_recv.at[h, idx], sibling).wait_recv()

    def q_copy():
        return remote(q_buf.at[max(off, 0)], q_buf.at[heads], q_send, q_recv, dev(2 * mate + y, tp))

    def position_column(row):
        line = pos_all[row]
        square = (rows, rows)
        same = lax.broadcasted_iota(jnp.int32, square, 0) == lax.broadcasted_iota(jnp.int32, square, 1)
        return jnp.sum(jnp.where(same, jnp.broadcast_to(line, square), 0), -1, keepdims=True)

    def attend(h, blocks, last):
        def one(turn, _):
            k = slots(h) - 1 - turn
            e = h + k * (heads - h)
            allowed = [
                jnp.concatenate([pos_all[2 * idx], pos_all[2 * idx + 1]], axis=1) <= q_pos[k] for idx in blocks
            ]
            values = [kv_buf[h, idx, :, :, pl.ds(wide, wide)].reshape(2 * rows, wide) for idx in blocks]
            fresh = []
            for a in range(2):
                query = q_buf[e, :, pl.ds(a * depth, depth)]
                scores = []
                for idx, mask in zip(blocks, allowed):
                    key = kv_buf[h, idx, :, :, pl.ds(a * depth, depth)].reshape(2 * rows, depth)
                    raw = lax.dot_general(
                        query, key, (((1,), (1,)), ((), ())), preferred_element_type=jnp.float32
                    )
                    scores.append(jnp.where(mask, raw, MASKED))
                before = high[e, a]
                now = before
                for part_scores in scores:
                    now = jnp.maximum(now, jnp.max(part_scores, -1, keepdims=True))
                keep = jnp.exp2((before - now) * scale)
                sums = total[e, a] * keep
                held = acc[e, a] * jnp.concatenate([keep] * (wide // 128), axis=1)
                for part_scores, value in zip(scores, values):
                    expo = jnp.exp2((part_scores - now[:, :1]) * scale)
                    sums = sums + jnp.sum(expo, -1, keepdims=True)
                    held = held + jnp.dot(expo.astype(jnp.bfloat16), value, preferred_element_type=jnp.float32)
                fresh.append((now, sums, held))
            for a in range(2):
                high[e, a], total[e, a], acc[e, a] = fresh[a]

            @pl.when(last)
            def _():
                finish(h, k)

            return 0

        lax.fori_loop(0, slots(h), one, 0)

    def head_columns(h):
        return pl.ds(pl.multiple_of(h * wide, wide), wide)

    def o_copy(h, k):
        e = h + k * (heads - h)
        to = dev(2 * (w + k * (mate - w)) + c, 2 * x + y)
        return remote(stage.at[e], normed.at[:, head_columns(h)], o_send.at[e], o_recv.at[h], to)

    def finish(h, k):
        e = h + k * (heads - h)
        first = acc[e, 0] / total[e, 0, :, :1]
        second = acc[e, 1] / total[e, 1, :, :1]
        diff = first - lam_wide[h] * second
        mean_square = jnp.mean(diff * diff, -1, keepdims=True)
        result = (out_factor * diff * lax.rsqrt(mean_square + norm_eps) * gain_wide[h]).astype(jnp.bfloat16)

        @pl.when(straight & (k == 0))
        def _():
            normed[:, head_columns(h)] = result

        @pl.when(crossed | (k > 0))
        def _():
            stage[e] = result
            o_copy(h, k).start()

    res_copy.start()

    high[...] = jnp.full(high.shape, LOWEST, jnp.float32)
    total[...] = jnp.zeros(total.shape, jnp.float32)
    acc[...] = jnp.zeros(acc.shape, jnp.float32)

    def step(t, _):
        s, h = lax.div(t, heads), lax.rem(t, heads)

        @pl.when(s == 0)
        def _():
            for way in range(2):

                @pl.when(straight & goes(way, h))
                def _():
                    pace(way, t)
                    to = dev(ctx + (2 if way else -2), tp)
                    own = pl.ds(pl.multiple_of(h * wide, wide), wide)
                    for j, src in enumerate((k_in, v_in)):
                        dst = kv_buf.at[h, w, y, :, pl.ds(j * wide, wide)]
                        remote(src.at[:, own], dst, line_send.at[way, h, w], line_recv.at[h, w], to).start()

            cols = pl.ds(0, wide)
            src = k_in.at[:, cols]
            pltpu.make_async_copy(src, kv_buf.at[h, w, c, :, cols], init_recv.at[h, 0]).wait()
            pltpu.make_async_copy(src, kv_buf.at[h, w, c, :, pl.ds(wide, wide)], init_recv.at[h, 1]).wait()

            for way in range(2):

                @pl.when(crossed & goes(way, h))
                def _():
                    pace(way, t)
                    line_copy(h, w, way).start()

            @pl.when(jnp.logical_not(left_out(h)))
            def _():
                sib_copy(h, w).start()

            pltpu.make_async_copy(src, q_buf.at[h], init_recv.at[h, 2]).wait()
            for later in range(2, heads):

                @pl.when(h == later - 2)
                def _():
                    init_start(later)

            @pl.when(left_out(h))
            def _():
                q_copy().start()

        @pl.when(t == heads)
        def _():
            for j, (src, dst) in enumerate(small_pairs):
                pltpu.make_async_copy(src, dst, small_recv.at[j]).wait()
            vecs = lam_buf[...]
            lam = (
                jnp.exp(jnp.sum(vecs[:, 0] * vecs[:, 1], -1, keepdims=True))
                - jnp.exp(jnp.sum(vecs[:, 2] * vecs[:, 3], -1, keepdims=True))
                + lambda_init
            )
            for i in range(heads):
                lam_wide[i] = jnp.broadcast_to(lam[i : i + 1], (1, wide))
                gain_wide[i] = jnp.concatenate([gain_buf[pl.ds(2 * i, 1)], gain_buf[pl.ds(2 * i + 1, 1)]], axis=1)

        @pl.when((s > 0) & (s < W) & jnp.logical_not(left_out(h)))
        def _():
            for way, idx in ((1, w - s), (0, w + s)):

                @pl.when((idx >= 0) & (idx < W))
                def _():
                    line_copy(h, idx, way).wait_recv()
                    sib_copy(h, idx).start()

            for way, idx in ((1, w - s), (0, w + s)):

                @pl.when((idx >= 0) & (idx < W) & goes(way, h))
                def _():
                    pace(way, t)
                    line_copy(h, idx, way).start()

        lax.fori_loop(
            jnp.clip((t - 1) * w_per_step, 0, w_total), jnp.clip(t * w_per_step, 0, w_total), w_start, 0
        )

        @pl.when(t == 1)
        def _():
            def pos_wait(i, _):
                frm = lax.rem(ctx + i, n_ctx)
                remote(pos_in, pos_all.at[frm], pos_send.at[i], pos_recv.at[frm], sibling).wait_recv()
                return 0

            pltpu.make_async_copy(pos_in, pos_all.at[ctx], pos_recv.at[ctx]).wait()
            lax.fori_loop(1, n_ctx, pos_wait, 0)
            q_pos[0] = jnp.broadcast_to(position_column(2 * w + c), q_pos.shape[1:])
            q_pos[1] = jnp.broadcast_to(position_column(2 * mate + c), q_pos.shape[1:])

        s1, h1 = lax.div(t + heads - 1, heads) - 1, lax.rem(t + heads - 1, heads)

        @pl.when((t > 0) & jnp.logical_not(left_out(h1)))
        def _():
            @pl.when(helper & (t == off + 1))
            def _():
                q_copy().wait_recv()

            last = s1 == jnp.maximum(w, W - 1 - w)
            on_left, on_right = w - s1 >= 0, (s1 > 0) & (w + s1 < W)

            @pl.when(on_left & on_right)
            def _():
                sib_wait(h1, w - s1)
                sib_wait(h1, w + s1)
                attend(h1, (w - s1, w + s1), last)

            @pl.when(on_left != on_right)
            def _():
                idx = jnp.where(on_left, w - s1, w + s1)
                sib_wait(h1, idx)
                attend(h1, (idx,), last)

        return 0

    lax.fori_loop(0, W * heads + 1, step, 0)

    for h in range(heads):

        @pl.when(crossed | left_out(h))
        def _():
            o_copy(h, 0).wait_recv()

    def product(i, core, j):
        target = 2 * lax.rem(x + i, X) + core
        w_copy(target, j).wait()
        return jnp.dot(normed[...], w_buf[target, j], preferred_element_type=jnp.float32)

    def ps_copy(i, j):
        return remote(part_sib.at[i, j], got_sib.at[i, j], ps_send.at[i, j], ps_recv.at[i, j], sibling)

    def p_copy(i, j):
        to = dev(ctx, 2 * lax.rem(x + i, X) + c)
        return remote(part.at[i - 1, j], got.at[i - 1, j], p_send.at[i - 1, j], p_recv.at[i - 1, j], to)

    def give_sibling(i):
        def body(j, _):
            part_sib[i, j] = product(i, 1 - c, j).astype(jnp.bfloat16)
            ps_copy(i, j).start()
            return 0

        lax.fori_loop(0, n_chunk, body, 0)

    def pair_sum(i, j):
        mine = product(i, c, j)
        ps_copy(i, j).wait_recv()
        return mine + got_sib[i, j].astype(jnp.float32)

    for i in range(1, X):

        def send_chunk(j, _):
            @pl.when(j < n_chunk)
            def _():
                part_sib[i, j] = product(i, 1 - c, j).astype(jnp.bfloat16)
                ps_copy(i, j).start()

            @pl.when(j >= 2)
            def _():
                part[i - 1, j - 2] = pair_sum(i, j - 2).astype(jnp.bfloat16)
                p_copy(i, j - 2).start()

            return 0

        lax.fori_loop(0, n_chunk + 2, send_chunk, 0)
    give_sibling(0)
    res_copy.wait()

    def pos_done(i, _):
        pos_copy(i).wait_send()
        return 0

    lax.fori_loop(1, n_ctx, pos_done, 0)

    @pl.when(crossed)
    def _():
        for h in range(heads):
            for j, (src, dst) in enumerate(init_pairs(h)):
                remote(src, dst, init_send.at[h, j], init_recv.at[h, j], partner).wait_send()

            @pl.when(jnp.logical_not(left_out(h)))
            def _():
                o_copy(h, 0).wait_send()

        for j, (src, dst) in enumerate(small_pairs):
            remote(src, dst, small_send.at[j], small_recv.at[j], partner).wait_send()

    @pl.when(helper)
    def _():
        o_copy(max(off, 0), 1).wait_send()

    @pl.when(at_end)
    def _():
        q_copy().wait_send()

    def line_done(idx, _):
        for h in range(heads):

            @pl.when(jnp.logical_not(left_out(h)))
            def _():
                sib_copy(h, idx).wait_send()

        return 0

    lax.fori_loop(0, W, line_done, 0)

    def piece_done(t, _):
        for way in range(2):
            h, idx, there = piece(way, t)

            @pl.when(there & jnp.logical_not(piece(way, t + 2)[2]))
            def _():
                line_copy(h, idx, way).wait_send()

        return 0

    lax.fori_loop(0, W * heads, piece_done, 0)

    def last_chunk(j, _):
        cols = pl.ds(pl.multiple_of(j * CHUNK, CHUNK), CHUNK)
        result = pair_sum(0, j) + res_buf[:, cols].astype(jnp.float32)
        for i in range(1, X):
            p_copy(i, j).wait()
            result = result + got[i - 1, j].astype(jnp.float32)
        for i in range(X):
            ps_copy(i, j).wait_send()
        out_ref[:, cols] = result.astype(out_ref.dtype)
        return 0

    lax.fori_loop(0, n_chunk, last_chunk, 0)


def per_device(n_ctx, n_tp, queries, keys, values, positions, lambda_vecs, head_gain, out_weight, residual):
    rows = queries.shape[0]
    heads, depth = lambda_vecs.shape[1], lambda_vecs.shape[2]
    wide = 2 * depth
    W, X = n_ctx // 2, n_tp // 2
    columns = out_weight.shape[1] // n_tp
    n_chunk = columns // CHUNK
    vmem = pl.BlockSpec(memory_space=pltpu.VMEM)
    hbm = pl.BlockSpec(memory_space=pl.ANY)
    bf16, f32 = jnp.bfloat16, jnp.float32
    dma = pltpu.SemaphoreType.DMA
    return pl.pallas_call(
        functools.partial(layer_kernel, n_ctx, n_tp),
        out_shape=jax.ShapeDtypeStruct((rows, columns), bf16),
        in_specs=[hbm] * 8,
        out_specs=vmem,
        scratch_shapes=[
            pltpu.VMEM((heads + 1, rows, wide), bf16),
            pltpu.VMEM((heads, W, 2, rows, 2 * wide), bf16),
            pltpu.VMEM((n_ctx, 1, rows), jnp.int32),
            pltpu.VMEM((heads, 4, depth), f32),
            pltpu.VMEM((2 * heads, depth), f32),
            pltpu.VMEM((heads, 1, wide), f32),
            pltpu.VMEM((heads, 1, wide), f32),
            pltpu.VMEM((2, rows, 2 * rows), jnp.int32),
            pltpu.VMEM((heads + 1, 2, rows, 128), f32),
            pltpu.VMEM((heads + 1, 2, rows, 128), f32),
            pltpu.VMEM((heads + 1, 2, rows, wide), f32),
            pltpu.VMEM((heads + 1, rows, wide), bf16),
            pltpu.VMEM((rows, heads * wide), bf16),
            pltpu.VMEM((n_tp, n_chunk, heads * wide, CHUNK), bf16),
            pltpu.VMEM((rows, columns), bf16),
            pltpu.VMEM((X, n_chunk, rows, CHUNK), bf16),
            pltpu.VMEM((X, n_chunk, rows, CHUNK), bf16),
            pltpu.VMEM((X - 1, n_chunk, rows, CHUNK), bf16),
            pltpu.VMEM((X - 1, n_chunk, rows, CHUNK), bf16),
            dma((heads, 3)),
            dma((heads, 3)),
            dma((2,)),
            dma((2,)),
            dma((n_ctx,)),
            dma((n_ctx,)),
            dma((2, heads, W)),
            dma((heads, W)),
            dma((heads, W)),
            dma((heads, W)),
            dma(()),
            dma(()),
            dma((heads + 1,)),
            dma((heads,)),
            dma((n_tp, n_chunk)),
            dma(()),
            dma((X, n_chunk)),
            dma((X, n_chunk)),
            dma((X - 1, n_chunk)),
            dma((X - 1, n_chunk)),
        ],
        compiler_params=pltpu.CompilerParams(
            collective_id=0, has_side_effects=True, vmem_limit_bytes=56 * 1024 * 1024
        ),
        name="attend_and_project",
    )(
        queries,
        keys,
        values,
        positions.reshape(1, rows),
        jnp.transpose(lambda_vecs, (1, 0, 2)),
        head_gain.reshape(2 * heads, depth),
        out_weight,
        residual,
    )


def solution(mesh):
    placed = (
        P("ctx", "tp"),
        P("ctx", "tp"),
        P("ctx", "tp"),
        P("ctx"),
        P(None, "tp", None),
        P("tp"),
        P("tp", None),
        P("ctx", "tp"),
    )
    return jax.shard_map(
        functools.partial(per_device, mesh.shape["ctx"], mesh.shape["tp"]),
        mesh=mesh,
        in_specs=placed,
        out_specs=P("ctx", "tp"),
        check_vma=False,
    )
```

```python
import functools
import math

import jax
import jax.numpy as jnp
from jax import lax
from jax.experimental import pallas as pl
from jax.experimental.pallas import tpu as pltpu
from jax.sharding import PartitionSpec as P

lambda_init = 0.2
out_factor = 0.8
norm_eps = 1e-05
MASKED = -3e38
LOWEST = -1e30


def column_cuts(columns):
    edges = [0] + list(range(256, columns, 512)) + [columns]
    return list(zip(edges[:-1], edges[1:]))


def layer_kernel(
    n_ctx,
    n_tp,
    q_in,
    k_in,
    v_in,
    pos_in,
    lam_in,
    gain_in,
    w_in,
    res_in,
    out_ref,
    q_buf,
    kv_buf,
    pos_all,
    lam_buf,
    gain_buf,
    lam_wide,
    gain_wide,
    q_pos,
    high,
    total,
    acc,
    stage,
    normed,
    w_buf,
    res_buf,
    base,
    part_sib,
    got_sib,
    part,
    got,
    init_send,
    init_recv,
    small_send,
    small_recv,
    pos_send,
    pos_recv,
    line_send,
    line_recv,
    sib_send,
    sib_recv,
    q_send,
    q_recv,
    o_send,
    o_recv,
    w_sem,
    res_sem,
    ps_send,
    ps_recv,
    p_send,
    p_recv,
):
    heads, rows, wide = stage.shape
    heads -= 1
    depth = wide // 2
    W = n_ctx // 2
    X = n_tp // 2
    columns = w_buf.shape[2]
    cuts = column_cuts(columns)
    off = heads - 1 if W >= 4 else -1
    scale = math.log2(math.e) / math.sqrt(depth)
    ctx = lax.axis_index("ctx")
    tp = lax.axis_index("tp")
    w, y = lax.div(ctx, 2), lax.rem(ctx, 2)
    x, c = lax.div(tp, 2), lax.rem(tp, 2)
    crossed = c != y
    straight = c == y
    at_end = (off >= 0) & ((w == 0) | (w == W - 1))
    helper = (off >= 0) & ((w == 1) | (w == W - 2))
    mate = jnp.where(w == 0, 1, jnp.where(w == W - 1, W - 2, jnp.where(w == 1, 0, jnp.where(w == W - 2, W - 1, w))))

    def left_out(h):
        return at_end & (h == off)

    def goes(way, h):
        if way:
            return (w < W - 1) & ((w != W - 2) | (h != off))
        return (w > 0) & ((w != 1) | (h != off))

    def slots(h):
        return 1 + jnp.where(helper & (h == off), 1, 0)

    def dev(a, b):
        return {"ctx": a, "tp": b}

    def remote(src, dst, send, recv, to):
        return pltpu.make_async_remote_copy(
            src_ref=src, dst_ref=dst, send_sem=send, recv_sem=recv, device_id=to, device_id_type=pl.DeviceIdType.MESH
        )

    partner = dev(2 * w + c, 2 * x + y)
    sibling = dev(ctx, 2 * x + 1 - c)
    far = dev(2 * mate + c, 2 * x + y)

    barrier = pltpu.get_barrier_semaphore()

    def greet(to):
        pl.semaphore_signal(barrier, inc=1, device_id=to, device_id_type=pl.DeviceIdType.MESH)

    greet(sibling)

    @pl.when(crossed)
    def _():
        greet(partner)

    @pl.when(crossed & (at_end | helper))
    def _():
        greet(far)

    for i in range(1, X):
        greet(dev(ctx, 2 * lax.rem(x + i, X) + c))

    def greet_row(i, _):
        greet(dev(lax.rem(ctx + i, n_ctx), tp))
        return 0

    lax.fori_loop(1, n_ctx, greet_row, 0)
    pl.semaphore_wait(barrier, n_ctx - 1 + 1 + X - 1 + lax.rem(c + y, 2) + jnp.where(crossed & (at_end | helper), 1, 0))

    def init_pairs(h):
        cols = pl.ds(h * wide, wide)
        return (
            (k_in.at[:, cols], kv_buf.at[h, w, y, :, pl.ds(0, wide)]),
            (v_in.at[:, cols], kv_buf.at[h, w, y, :, pl.ds(wide, wide)]),
            (q_in.at[:, cols], q_buf.at[h]),
        )

    small_pairs = ((lam_in, lam_buf), (gain_in, gain_buf))

    def init_start(h):
        @pl.when(straight)
        def _():
            for j, (src, dst) in enumerate(init_pairs(h)):
                pltpu.make_async_copy(src, dst, init_recv.at[h, j]).start()

        @pl.when(crossed)
        def _():
            for j, (src, dst) in enumerate(init_pairs(h)):
                remote(src, dst, init_send.at[h, j], init_recv.at[h, j], partner).start()

    for h in range(min(2, heads)):
        init_start(h)

    @pl.when(straight)
    def _():
        for j, (src, dst) in enumerate(small_pairs):
            pltpu.make_async_copy(src, dst, small_recv.at[j]).start()

    @pl.when(crossed)
    def _():
        for j, (src, dst) in enumerate(small_pairs):
            remote(src, dst, small_send.at[j], small_recv.at[j], partner).start()

    def pos_copy(i):
        return remote(
            pos_in,
            pos_all.at[ctx],
            pos_send.at[i],
            pos_recv.at[ctx],
            dev(lax.rem(ctx + i, n_ctx), tp),
        )

    def pos_start(i, _):
        pos_copy(i).start()
        return 0

    pltpu.make_async_copy(pos_in, pos_all.at[ctx], pos_recv.at[ctx]).start()
    lax.fori_loop(1, n_ctx, pos_start, 0)

    def w_copy(i):
        start = pl.multiple_of(i * columns, 128)
        return pltpu.make_async_copy(w_in.at[:, pl.ds(start, columns)], w_buf.at[i], w_sem.at[i])

    def w_start(k, _):
        i, core = lax.rem(lax.div(k, 2) + x + 1, X), lax.rem(k + c + 1, 2)
        w_copy(2 * i + core).start()
        return 0

    res_copy = pltpu.make_async_copy(res_in, res_buf, res_sem)

    def line_copy(h, idx, way):
        block = kv_buf.at[h, idx, c]
        to = dev(ctx + (2 if way else -2), tp)
        return remote(block, block, line_send.at[way, h, idx], line_recv.at[h, idx], to)

    def piece(way, t):
        s, h = lax.div(t + heads, heads) - 1, lax.rem(t + heads, heads)
        idx = w - s if way else w + s
        return h, idx, (s >= 0) & (idx >= 0) & (idx < W) & goes(way, h)

    def pace(way, t):
        h, idx, there = piece(way, t - 2)

        @pl.when(there)
        def _():
            line_copy(h, idx, way).wait_send()

    def sib_copy(h, idx):
        block = kv_buf.at[h, idx, c]
        return remote(block, block, sib_send.at[h, idx], sib_recv.at[h, idx], sibling)

    def sib_wait(h, idx):
        block = kv_buf.at[h, idx, 1 - c]
        remote(block, block, sib_send.at[h, idx], sib_recv.at[h, idx], sibling).wait_recv()

    def q_copy():
        return remote(q_buf.at[max(off, 0)], q_buf.at[heads], q_send, q_recv, dev(2 * mate + y, tp))

    def position_column(row):
        line = pos_all[row]
        square = (rows, rows)
        same = lax.broadcasted_iota(jnp.int32, square, 0) == lax.broadcasted_iota(jnp.int32, square, 1)
        return jnp.sum(jnp.where(same, jnp.broadcast_to(line, square), 0), -1, keepdims=True)

    def attend(h, blocks, last):
        def one(turn, _):
            k = slots(h) - 1 - turn
            e = h + k * (heads - h)
            allowed = [
                jnp.concatenate([pos_all[2 * idx], pos_all[2 * idx + 1]], axis=1) <= q_pos[k] for idx in blocks
            ]
            values = [kv_buf[h, idx, :, :, pl.ds(wide, wide)].reshape(2 * rows, wide) for idx in blocks]
            fresh = []
            for a in range(2):
                query = q_buf[e, :, pl.ds(a * depth, depth)]
                scores = []
                for idx, mask in zip(blocks, allowed):
                    key = kv_buf[h, idx, :, :, pl.ds(a * depth, depth)].reshape(2 * rows, depth)
                    raw = lax.dot_general(
                        query, key, (((1,), (1,)), ((), ())), preferred_element_type=jnp.float32
                    )
                    scores.append(jnp.where(mask, raw, MASKED))
                before = high[e, a]
                now = before
                for part_scores in scores:
                    now = jnp.maximum(now, jnp.max(part_scores, -1, keepdims=True))
                keep = jnp.exp2((before - now) * scale)
                sums = total[e, a] * keep
                held = acc[e, a] * jnp.concatenate([keep] * (wide // 128), axis=1)
                for part_scores, value in zip(scores, values):
                    expo = jnp.exp2((part_scores - now[:, :1]) * scale)
                    sums = sums + jnp.sum(expo, -1, keepdims=True)
                    held = held + jnp.dot(expo.astype(jnp.bfloat16), value, preferred_element_type=jnp.float32)
                fresh.append((now, sums, held))
            for a in range(2):
                high[e, a], total[e, a], acc[e, a] = fresh[a]

            @pl.when(last)
            def _():
                finish(h, k)

            return 0

        lax.fori_loop(0, slots(h), one, 0)

    def head_columns(h):
        return pl.ds(pl.multiple_of(h * wide, wide), wide)

    def o_copy(h, k):
        e = h + k * (heads - h)
        to = dev(2 * (w + k * (mate - w)) + c, 2 * x + y)
        return remote(stage.at[e], normed.at[:, head_columns(h)], o_send.at[e], o_recv.at[h], to)

    def finish(h, k):
        e = h + k * (heads - h)
        first = acc[e, 0] / total[e, 0, :, :1]
        second = acc[e, 1] / total[e, 1, :, :1]
        diff = first - lam_wide[h] * second
        mean_square = jnp.mean(diff * diff, -1, keepdims=True)
        result = (out_factor * diff * lax.rsqrt(mean_square + norm_eps) * gain_wide[h]).astype(jnp.bfloat16)

        @pl.when(straight & (k == 0))
        def _():
            normed[:, head_columns(h)] = result

        @pl.when(crossed | (k > 0))
        def _():
            stage[e] = result
            o_copy(h, k).start()

    res_copy.start()

    high[...] = jnp.full(high.shape, LOWEST, jnp.float32)
    total[...] = jnp.zeros(total.shape, jnp.float32)
    acc[...] = jnp.zeros(acc.shape, jnp.float32)

    def step(t, _):
        s, h = lax.div(t, heads), lax.rem(t, heads)

        @pl.when(s == 0)
        def _():
            for way in range(2):

                @pl.when(straight & goes(way, h))
                def _():
                    pace(way, t)
                    to = dev(ctx + (2 if way else -2), tp)
                    own = pl.ds(pl.multiple_of(h * wide, wide), wide)
                    for j, src in enumerate((k_in, v_in)):
                        dst = kv_buf.at[h, w, y, :, pl.ds(j * wide, wide)]
                        remote(src.at[:, own], dst, line_send.at[way, h, w], line_recv.at[h, w], to).start()

            cols = pl.ds(0, wide)
            src = k_in.at[:, cols]
            pltpu.make_async_copy(src, kv_buf.at[h, w, c, :, cols], init_recv.at[h, 0]).wait()
            pltpu.make_async_copy(src, kv_buf.at[h, w, c, :, pl.ds(wide, wide)], init_recv.at[h, 1]).wait()

            for way in range(2):

                @pl.when(crossed & goes(way, h))
                def _():
                    pace(way, t)
                    line_copy(h, w, way).start()

            @pl.when(jnp.logical_not(left_out(h)))
            def _():
                sib_copy(h, w).start()

            pltpu.make_async_copy(src, q_buf.at[h], init_recv.at[h, 2]).wait()
            for later in range(2, heads):

                @pl.when(h == later - 2)
                def _():
                    init_start(later)

            @pl.when(left_out(h))
            def _():
                q_copy().start()

        @pl.when(t == heads)
        def _():
            for j, (src, dst) in enumerate(small_pairs):
                pltpu.make_async_copy(src, dst, small_recv.at[j]).wait()
            vecs = lam_buf[...]
            lam = (
                jnp.exp(jnp.sum(vecs[:, 0] * vecs[:, 1], -1, keepdims=True))
                - jnp.exp(jnp.sum(vecs[:, 2] * vecs[:, 3], -1, keepdims=True))
                + lambda_init
            )
            for i in range(heads):
                lam_wide[i] = jnp.broadcast_to(lam[i : i + 1], (1, wide))
                gain_wide[i] = jnp.concatenate([gain_buf[pl.ds(2 * i, 1)], gain_buf[pl.ds(2 * i + 1, 1)]], axis=1)

        @pl.when((s > 0) & (s < W) & jnp.logical_not(left_out(h)))
        def _():
            for way, idx in ((1, w - s), (0, w + s)):

                @pl.when((idx >= 0) & (idx < W))
                def _():
                    line_copy(h, idx, way).wait_recv()
                    sib_copy(h, idx).start()

            for way, idx in ((1, w - s), (0, w + s)):

                @pl.when((idx >= 0) & (idx < W) & goes(way, h))
                def _():
                    pace(way, t)
                    line_copy(h, idx, way).start()

        lax.fori_loop(jnp.clip(t - 1, 0, n_tp), jnp.clip(t, 0, n_tp), w_start, 0)

        @pl.when(t == 1)
        def _():
            def pos_wait(i, _):
                frm = lax.rem(ctx + i, n_ctx)
                remote(pos_in, pos_all.at[frm], pos_send.at[i], pos_recv.at[frm], sibling).wait_recv()
                return 0

            pltpu.make_async_copy(pos_in, pos_all.at[ctx], pos_recv.at[ctx]).wait()
            lax.fori_loop(1, n_ctx, pos_wait, 0)
            q_pos[0] = jnp.broadcast_to(position_column(2 * w + c), q_pos.shape[1:])
            q_pos[1] = jnp.broadcast_to(position_column(2 * mate + c), q_pos.shape[1:])

        s1, h1 = lax.div(t + heads - 1, heads) - 1, lax.rem(t + heads - 1, heads)

        @pl.when((t > 0) & jnp.logical_not(left_out(h1)))
        def _():
            @pl.when(helper & (t == off + 1))
            def _():
                q_copy().wait_recv()

            last = s1 == jnp.maximum(w, W - 1 - w)
            on_left, on_right = w - s1 >= 0, (s1 > 0) & (w + s1 < W)

            @pl.when(on_left & on_right)
            def _():
                sib_wait(h1, w - s1)
                sib_wait(h1, w + s1)
                attend(h1, (w - s1, w + s1), last)

            @pl.when(on_left != on_right)
            def _():
                idx = jnp.where(on_left, w - s1, w + s1)
                sib_wait(h1, idx)
                attend(h1, (idx,), last)

        return 0

    lax.fori_loop(0, W * heads + 1, step, 0)

    for h in range(heads):

        @pl.when(crossed | left_out(h))
        def _():
            o_copy(h, 0).wait_recv()

    def product(i, core, lo, hi):
        target = 2 * lax.rem(x + i, X) + core
        return jnp.dot(normed[...], w_buf[target, :, lo:hi], preferred_element_type=jnp.float32)

    def w_wait(i, core):
        w_copy(2 * lax.rem(x + i, X) + core).wait()

    def ps_copy(i, j, lo, hi):
        cols = pl.ds(lo, hi - lo)
        return remote(part_sib.at[i, :, cols], got_sib.at[i, :, cols], ps_send.at[i, j], ps_recv.at[i, j], sibling)

    def p_copy(i, j):
        lo, hi = cuts[j]
        cols = pl.ds(lo, hi - lo)
        to = dev(ctx, 2 * lax.rem(x + i, X) + c)
        return remote(
            part.at[i - 1, :, cols], got.at[i - 1, :, cols], p_send.at[i - 1, j], p_recv.at[i - 1, j], to
        )

    def give_sibling(i, j, lo, hi):
        part_sib[i, :, lo:hi] = product(i, 1 - c, lo, hi).astype(jnp.bfloat16)
        ps_copy(i, j, lo, hi).start()

    for i in range(1, X):
        w_wait(i, 1 - c)
        w_wait(i, c)
        for j in range(len(cuts) + 1):
            if j < len(cuts):
                give_sibling(i, j, *cuts[j])
            if j >= 1:
                lo, hi = cuts[j - 1]
                mine = product(i, c, lo, hi)
                ps_copy(i, j - 1, lo, hi).wait_recv()
                part[i - 1, :, lo:hi] = (mine + got_sib[i, :, lo:hi].astype(jnp.float32)).astype(jnp.bfloat16)
                p_copy(i, j - 1).start()
    w_wait(0, 1 - c)
    w_wait(0, c)
    give_sibling(0, 0, 0, columns)
    res_copy.wait()
    base[...] = product(0, c, 0, columns) + res_buf[...].astype(jnp.float32)

    def pos_done(i, _):
        pos_copy(i).wait_send()
        return 0

    lax.fori_loop(1, n_ctx, pos_done, 0)

    @pl.when(crossed)
    def _():
        for h in range(heads):
            for j, (src, dst) in enumerate(init_pairs(h)):
                remote(src, dst, init_send.at[h, j], init_recv.at[h, j], partner).wait_send()

            @pl.when(jnp.logical_not(left_out(h)))
            def _():
                o_copy(h, 0).wait_send()

        for j, (src, dst) in enumerate(small_pairs):
            remote(src, dst, small_send.at[j], small_recv.at[j], partner).wait_send()

    @pl.when(helper)
    def _():
        o_copy(max(off, 0), 1).wait_send()

    @pl.when(at_end)
    def _():
        q_copy().wait_send()

    def line_done(idx, _):
        for h in range(heads):

            @pl.when(jnp.logical_not(left_out(h)))
            def _():
                sib_copy(h, idx).wait_send()

        return 0

    lax.fori_loop(0, W, line_done, 0)

    def piece_done(t, _):
        for way in range(2):
            h, idx, there = piece(way, t)

            @pl.when(there & jnp.logical_not(piece(way, t + 2)[2]))
            def _():
                line_copy(h, idx, way).wait_send()

        return 0

    lax.fori_loop(0, W * heads, piece_done, 0)

    ps_copy(0, 0, 0, columns).wait()
    for i in range(1, X):
        for j, (lo, hi) in enumerate(cuts):
            ps_copy(i, j, lo, hi).wait_send()
    for j, (lo, hi) in enumerate(cuts):
        result = base[:, lo:hi] + got_sib[0, :, lo:hi].astype(jnp.float32)
        for i in range(1, X):
            p_copy(i, j).wait()
            result = result + got[i - 1, :, lo:hi].astype(jnp.float32)
        out_ref[:, lo:hi] = result.astype(out_ref.dtype)


def per_device(n_ctx, n_tp, queries, keys, values, positions, lambda_vecs, head_gain, out_weight, residual):
    rows = queries.shape[0]
    heads, depth = lambda_vecs.shape[1], lambda_vecs.shape[2]
    wide = 2 * depth
    W, X = n_ctx // 2, n_tp // 2
    columns = out_weight.shape[1] // n_tp
    n_cut = len(column_cuts(columns))
    vmem = pl.BlockSpec(memory_space=pltpu.VMEM)
    hbm = pl.BlockSpec(memory_space=pl.ANY)
    bf16, f32 = jnp.bfloat16, jnp.float32
    dma = pltpu.SemaphoreType.DMA
    return pl.pallas_call(
        functools.partial(layer_kernel, n_ctx, n_tp),
        out_shape=jax.ShapeDtypeStruct((rows, columns), bf16),
        in_specs=[hbm] * 8,
        out_specs=vmem,
        scratch_shapes=[
            pltpu.VMEM((heads + 1, rows, wide), bf16),
            pltpu.VMEM((heads, W, 2, rows, 2 * wide), bf16),
            pltpu.VMEM((n_ctx, 1, rows), jnp.int32),
            pltpu.VMEM((heads, 4, depth), f32),
            pltpu.VMEM((2 * heads, depth), f32),
            pltpu.VMEM((heads, 1, wide), f32),
            pltpu.VMEM((heads, 1, wide), f32),
            pltpu.VMEM((2, rows, 2 * rows), jnp.int32),
            pltpu.VMEM((heads + 1, 2, rows, 128), f32),
            pltpu.VMEM((heads + 1, 2, rows, 128), f32),
            pltpu.VMEM((heads + 1, 2, rows, wide), f32),
            pltpu.VMEM((heads + 1, rows, wide), bf16),
            pltpu.VMEM((rows, heads * wide), bf16),
            pltpu.VMEM((n_tp, heads * wide, columns), bf16),
            pltpu.VMEM((rows, columns), bf16),
            pltpu.VMEM((rows, columns), f32),
            pltpu.VMEM((X, rows, columns), bf16),
            pltpu.VMEM((X, rows, columns), bf16),
            pltpu.VMEM((X - 1, rows, columns), bf16),
            pltpu.VMEM((X - 1, rows, columns), bf16),
            dma((heads, 3)),
            dma((heads, 3)),
            dma((2,)),
            dma((2,)),
            dma((n_ctx,)),
            dma((n_ctx,)),
            dma((2, heads, W)),
            dma((heads, W)),
            dma((heads, W)),
            dma((heads, W)),
            dma(()),
            dma(()),
            dma((heads + 1,)),
            dma((heads,)),
            dma((n_tp,)),
            dma(()),
            dma((X, n_cut)),
            dma((X, n_cut)),
            dma((X - 1, n_cut)),
            dma((X - 1, n_cut)),
        ],
        compiler_params=pltpu.CompilerParams(
            collective_id=0, has_side_effects=True, vmem_limit_bytes=56 * 1024 * 1024
        ),
        name="attend_and_project",
    )(
        queries,
        keys,
        values,
        positions.reshape(1, rows),
        jnp.transpose(lambda_vecs, (1, 0, 2)),
        head_gain.reshape(2 * heads, depth),
        out_weight,
        residual,
    )


def solution(mesh):
    placed = (
        P("ctx", "tp"),
        P("ctx", "tp"),
        P("ctx", "tp"),
        P("ctx"),
        P(None, "tp", None),
        P("tp"),
        P("tp", None),
        P("ctx", "tp"),
    )
    return jax.shard_map(
        functools.partial(per_device, mesh.shape["ctx"], mesh.shape["tp"]),
        mesh=mesh,
        in_specs=placed,
        out_specs=P("ctx", "tp"),
        check_vma=False,
    )
```

```python
import functools
import math

import jax
import jax.numpy as jnp
from jax import lax
from jax.experimental import pallas as pl
from jax.experimental.pallas import tpu as pltpu
from jax.sharding import PartitionSpec as P

lambda_init = 0.2
out_factor = 0.8
norm_eps = 1e-05
MASKED = -3e38
LOWEST = -1e30


def column_cuts(columns):
    edges = [0] + list(range(256, columns, 512)) + [columns]
    return list(zip(edges[:-1], edges[1:]))


def layer_kernel(
    n_ctx,
    n_tp,
    q_in,
    k_in,
    v_in,
    pos_in,
    lam_in,
    gain_in,
    w_in,
    res_in,
    out_ref,
    q_buf,
    kv_buf,
    pos_all,
    lam_buf,
    gain_buf,
    lam_wide,
    gain_wide,
    q_pos,
    high,
    total,
    acc,
    stage,
    normed,
    w_buf,
    res_buf,
    base,
    part_sib,
    got_sib,
    part,
    got,
    init_send,
    init_recv,
    small_send,
    small_recv,
    pos_send,
    pos_recv,
    line_send,
    line_recv,
    sib_send,
    sib_recv,
    q_send,
    q_recv,
    o_send,
    o_recv,
    w_sem,
    res_sem,
    ps_send,
    ps_recv,
    p_send,
    p_recv,
):
    heads, rows, wide = stage.shape
    heads -= 1
    depth = wide // 2
    W = n_ctx // 2
    X = n_tp // 2
    columns = w_buf.shape[2]
    cuts = column_cuts(columns)
    off = heads - 1 if W >= 4 else -1
    scale = math.log2(math.e) / math.sqrt(depth)
    ctx = lax.axis_index("ctx")
    tp = lax.axis_index("tp")
    w, y = lax.div(ctx, 2), lax.rem(ctx, 2)
    x, c = lax.div(tp, 2), lax.rem(tp, 2)
    crossed = c != y
    straight = c == y
    at_end = (off >= 0) & ((w == 0) | (w == W - 1))
    helper = (off >= 0) & ((w == 1) | (w == W - 2))
    mate = jnp.where(w == 0, 1, jnp.where(w == W - 1, W - 2, jnp.where(w == 1, 0, jnp.where(w == W - 2, W - 1, w))))

    def left_out(h):
        return at_end & (h == off)

    def goes(way, h):
        if way:
            return (w < W - 1) & ((w != W - 2) | (h != off))
        return (w > 0) & ((w != 1) | (h != off))

    def slots(h):
        return 1 + jnp.where(helper & (h == off), 1, 0)

    def dev(a, b):
        return {"ctx": a, "tp": b}

    def remote(src, dst, send, recv, to):
        return pltpu.make_async_remote_copy(
            src_ref=src, dst_ref=dst, send_sem=send, recv_sem=recv, device_id=to, device_id_type=pl.DeviceIdType.MESH
        )

    partner = dev(2 * w + c, 2 * x + y)
    sibling = dev(ctx, 2 * x + 1 - c)
    far = dev(2 * mate + c, 2 * x + y)

    def init_pairs(h):
        cols = pl.ds(h * wide, wide)
        return (
            (k_in.at[:, cols], kv_buf.at[h, w, y, :, pl.ds(0, wide)]),
            (v_in.at[:, cols], kv_buf.at[h, w, y, :, pl.ds(wide, wide)]),
            (q_in.at[:, cols], q_buf.at[h]),
        )

    small_pairs = ((lam_in, lam_buf), (gain_in, gain_buf))

    def w_copy(i):
        start = pl.multiple_of(i * columns, 128)
        return pltpu.make_async_copy(w_in.at[:, pl.ds(start, columns)], w_buf.at[i], w_sem.at[i])

    res_copy = pltpu.make_async_copy(res_in, res_buf, res_sem)

    @pl.when(straight)
    def _():
        for h in range(heads):
            for j, (src, dst) in enumerate(init_pairs(h)):
                pltpu.make_async_copy(src, dst, init_recv.at[h, j]).start()
        for j, (src, dst) in enumerate(small_pairs):
            pltpu.make_async_copy(src, dst, small_recv.at[j]).start()

    pltpu.make_async_copy(pos_in, pos_all.at[ctx], pos_recv.at[ctx]).start()
    for k in range(2 * X):
        w_copy(2 * lax.rem(x + k // 2 + 1, X) + lax.rem(c + k + 1, 2)).start()
    res_copy.start()

    barrier = pltpu.get_barrier_semaphore()

    def greet(to):
        pl.semaphore_signal(barrier, inc=1, device_id=to, device_id_type=pl.DeviceIdType.MESH)

    greet(sibling)

    @pl.when(crossed)
    def _():
        greet(partner)

    @pl.when(crossed & (at_end | helper))
    def _():
        greet(far)

    for i in range(1, X):
        greet(dev(ctx, 2 * lax.rem(x + i, X) + c))

    def greet_row(i, _):
        greet(dev(lax.rem(ctx + i, n_ctx), tp))
        return 0

    lax.fori_loop(1, n_ctx, greet_row, 0)
    pl.semaphore_wait(barrier, n_ctx - 1 + 1 + X - 1 + lax.rem(c + y, 2) + jnp.where(crossed & (at_end | helper), 1, 0))

    def init_start(h):
        @pl.when(crossed)
        def _():
            for j, (src, dst) in enumerate(init_pairs(h)):
                remote(src, dst, init_send.at[h, j], init_recv.at[h, j], partner).start()

    for h in range(min(2, heads)):
        init_start(h)

    @pl.when(crossed)
    def _():
        for j, (src, dst) in enumerate(small_pairs):
            remote(src, dst, small_send.at[j], small_recv.at[j], partner).start()

    def pos_copy(i):
        return remote(
            pos_in,
            pos_all.at[ctx],
            pos_send.at[i],
            pos_recv.at[ctx],
            dev(lax.rem(ctx + i, n_ctx), tp),
        )

    def pos_start(i, _):
        pos_copy(i).start()
        return 0

    lax.fori_loop(1, n_ctx, pos_start, 0)

    def line_copy(h, idx, way):
        block = kv_buf.at[h, idx, c]
        to = dev(ctx + (2 if way else -2), tp)
        return remote(block, block, line_send.at[way, h, idx], line_recv.at[h, idx], to)

    def piece(way, t):
        s, h = lax.div(t + heads, heads) - 1, lax.rem(t + heads, heads)
        idx = w - s if way else w + s
        return h, idx, (s >= 0) & (idx >= 0) & (idx < W) & goes(way, h)

    def pace(way, t):
        h, idx, there = piece(way, t - 2)

        @pl.when(there)
        def _():
            line_copy(h, idx, way).wait_send()

    def sib_copy(h, idx):
        block = kv_buf.at[h, idx, c]
        return remote(block, block, sib_send.at[h, idx], sib_recv.at[h, idx], sibling)

    def sib_wait(h, idx):
        block = kv_buf.at[h, idx, 1 - c]
        remote(block, block, sib_send.at[h, idx], sib_recv.at[h, idx], sibling).wait_recv()

    def q_copy():
        return remote(q_buf.at[max(off, 0)], q_buf.at[heads], q_send, q_recv, dev(2 * mate + y, tp))

    def position_column(row):
        line = pos_all[row]
        square = (rows, rows)
        same = lax.broadcasted_iota(jnp.int32, square, 0) == lax.broadcasted_iota(jnp.int32, square, 1)
        return jnp.sum(jnp.where(same, jnp.broadcast_to(line, square), 0), -1, keepdims=True)

    def attend(h, blocks, last):
        def one(turn, _):
            k = slots(h) - 1 - turn
            e = h + k * (heads - h)
            allowed = [
                jnp.concatenate([pos_all[2 * idx], pos_all[2 * idx + 1]], axis=1) <= q_pos[k] for idx in blocks
            ]
            values = [kv_buf[h, idx, :, :, pl.ds(wide, wide)].reshape(2 * rows, wide) for idx in blocks]
            fresh = []
            for a in range(2):
                query = q_buf[e, :, pl.ds(a * depth, depth)]
                scores = []
                for idx, mask in zip(blocks, allowed):
                    key = kv_buf[h, idx, :, :, pl.ds(a * depth, depth)].reshape(2 * rows, depth)
                    raw = lax.dot_general(
                        query, key, (((1,), (1,)), ((), ())), preferred_element_type=jnp.float32
                    )
                    scores.append(jnp.where(mask, raw, MASKED))
                before = high[e, a]
                now = before
                for part_scores in scores:
                    now = jnp.maximum(now, jnp.max(part_scores, -1, keepdims=True))
                keep = jnp.exp2((before - now) * scale)
                sums = total[e, a] * keep
                held = acc[e, a] * jnp.concatenate([keep] * (wide // 128), axis=1)
                for part_scores, value in zip(scores, values):
                    expo = jnp.exp2((part_scores - now[:, :1]) * scale)
                    sums = sums + jnp.sum(expo, -1, keepdims=True)
                    held = held + jnp.dot(expo.astype(jnp.bfloat16), value, preferred_element_type=jnp.float32)
                fresh.append((now, sums, held))
            for a in range(2):
                high[e, a], total[e, a], acc[e, a] = fresh[a]

            @pl.when(last)
            def _():
                finish(h, k)

            return 0

        lax.fori_loop(0, slots(h), one, 0)

    def head_columns(h):
        return pl.ds(pl.multiple_of(h * wide, wide), wide)

    def o_copy(h, k):
        e = h + k * (heads - h)
        to = dev(2 * (w + k * (mate - w)) + c, 2 * x + y)
        return remote(stage.at[e], normed.at[:, head_columns(h)], o_send.at[e], o_recv.at[h], to)

    def finish(h, k):
        e = h + k * (heads - h)
        first = acc[e, 0] / total[e, 0, :, :1]
        second = acc[e, 1] / total[e, 1, :, :1]
        diff = first - lam_wide[h] * second
        mean_square = jnp.mean(diff * diff, -1, keepdims=True)
        result = (out_factor * diff * lax.rsqrt(mean_square + norm_eps) * gain_wide[h]).astype(jnp.bfloat16)

        @pl.when(straight & (k == 0))
        def _():
            normed[:, head_columns(h)] = result

        @pl.when(crossed | (k > 0))
        def _():
            stage[e] = result
            o_copy(h, k).start()

    high[...] = jnp.full(high.shape, LOWEST, jnp.float32)
    total[...] = jnp.zeros(total.shape, jnp.float32)
    acc[...] = jnp.zeros(acc.shape, jnp.float32)

    def step(t, _):
        s, h = lax.div(t, heads), lax.rem(t, heads)

        @pl.when(s == 0)
        def _():
            for way in range(2):

                @pl.when(straight & goes(way, h))
                def _():
                    pace(way, t)
                    to = dev(ctx + (2 if way else -2), tp)
                    own = pl.ds(pl.multiple_of(h * wide, wide), wide)
                    for j, src in enumerate((k_in, v_in)):
                        dst = kv_buf.at[h, w, y, :, pl.ds(j * wide, wide)]
                        remote(src.at[:, own], dst, line_send.at[way, h, w], line_recv.at[h, w], to).start()

            cols = pl.ds(0, wide)
            src = k_in.at[:, cols]
            pltpu.make_async_copy(src, kv_buf.at[h, w, c, :, cols], init_recv.at[h, 0]).wait()
            pltpu.make_async_copy(src, kv_buf.at[h, w, c, :, pl.ds(wide, wide)], init_recv.at[h, 1]).wait()

            for way in range(2):

                @pl.when(crossed & goes(way, h))
                def _():
                    pace(way, t)
                    line_copy(h, w, way).start()

            @pl.when(jnp.logical_not(left_out(h)))
            def _():
                sib_copy(h, w).start()

            pltpu.make_async_copy(src, q_buf.at[h], init_recv.at[h, 2]).wait()
            for later in range(2, heads):

                @pl.when(h == later - 2)
                def _():
                    init_start(later)

            @pl.when(left_out(h))
            def _():
                q_copy().start()

        @pl.when(t == heads)
        def _():
            for j, (src, dst) in enumerate(small_pairs):
                pltpu.make_async_copy(src, dst, small_recv.at[j]).wait()
            vecs = lam_buf[...]
            lam = (
                jnp.exp(jnp.sum(vecs[:, 0] * vecs[:, 1], -1, keepdims=True))
                - jnp.exp(jnp.sum(vecs[:, 2] * vecs[:, 3], -1, keepdims=True))
                + lambda_init
            )
            for i in range(heads):
                lam_wide[i] = jnp.broadcast_to(lam[i : i + 1], (1, wide))
                gain_wide[i] = jnp.concatenate([gain_buf[pl.ds(2 * i, 1)], gain_buf[pl.ds(2 * i + 1, 1)]], axis=1)

        @pl.when((s > 0) & (s < W) & jnp.logical_not(left_out(h)))
        def _():
            for way, idx in ((1, w - s), (0, w + s)):

                @pl.when((idx >= 0) & (idx < W))
                def _():
                    line_copy(h, idx, way).wait_recv()
                    sib_copy(h, idx).start()

            for way, idx in ((1, w - s), (0, w + s)):

                @pl.when((idx >= 0) & (idx < W) & goes(way, h))
                def _():
                    pace(way, t)
                    line_copy(h, idx, way).start()

        @pl.when(t == 1)
        def _():
            def pos_wait(i, _):
                frm = lax.rem(ctx + i, n_ctx)
                remote(pos_in, pos_all.at[frm], pos_send.at[i], pos_recv.at[frm], sibling).wait_recv()
                return 0

            pltpu.make_async_copy(pos_in, pos_all.at[ctx], pos_recv.at[ctx]).wait()
            lax.fori_loop(1, n_ctx, pos_wait, 0)
            q_pos[0] = jnp.broadcast_to(position_column(2 * w + c), q_pos.shape[1:])
            q_pos[1] = jnp.broadcast_to(position_column(2 * mate + c), q_pos.shape[1:])

        s1, h1 = lax.div(t + heads - 1, heads) - 1, lax.rem(t + heads - 1, heads)

        @pl.when((t > 0) & jnp.logical_not(left_out(h1)))
        def _():
            @pl.when(helper & (t == off + 1))
            def _():
                q_copy().wait_recv()

            last = s1 == jnp.maximum(w, W - 1 - w)
            on_left, on_right = w - s1 >= 0, (s1 > 0) & (w + s1 < W)

            @pl.when(on_left & on_right)
            def _():
                sib_wait(h1, w - s1)
                sib_wait(h1, w + s1)
                attend(h1, (w - s1, w + s1), last)

            @pl.when(on_left != on_right)
            def _():
                idx = jnp.where(on_left, w - s1, w + s1)
                sib_wait(h1, idx)
                attend(h1, (idx,), last)

        return 0

    lax.fori_loop(0, W * heads + 1, step, 0)

    for h in range(heads):

        @pl.when(crossed | left_out(h))
        def _():
            o_copy(h, 0).wait_recv()

    def product(i, core, lo, hi):
        target = 2 * lax.rem(x + i, X) + core
        return jnp.dot(normed[...], w_buf[target, :, lo:hi], preferred_element_type=jnp.float32)

    def w_wait(i, core):
        w_copy(2 * lax.rem(x + i, X) + core).wait()

    def ps_copy(i, j, lo, hi):
        cols = pl.ds(lo, hi - lo)
        return remote(part_sib.at[i, :, cols], got_sib.at[i, :, cols], ps_send.at[i, j], ps_recv.at[i, j], sibling)

    def p_copy(i, j):
        lo, hi = cuts[j]
        cols = pl.ds(lo, hi - lo)
        to = dev(ctx, 2 * lax.rem(x + i, X) + c)
        return remote(
            part.at[i - 1, :, cols], got.at[i - 1, :, cols], p_send.at[i - 1, j], p_recv.at[i - 1, j], to
        )

    def give_sibling(i, j, lo, hi):
        part_sib[i, :, lo:hi] = product(i, 1 - c, lo, hi).astype(jnp.bfloat16)
        ps_copy(i, j, lo, hi).start()

    for i in range(1, X):
        w_wait(i, 1 - c)
        w_wait(i, c)
        for j in range(len(cuts) + 1):
            if j < len(cuts):
                give_sibling(i, j, *cuts[j])
            if j >= 1:
                lo, hi = cuts[j - 1]
                mine = product(i, c, lo, hi)
                ps_copy(i, j - 1, lo, hi).wait_recv()
                part[i - 1, :, lo:hi] = (mine + got_sib[i, :, lo:hi].astype(jnp.float32)).astype(jnp.bfloat16)
                p_copy(i, j - 1).start()
    w_wait(0, 1 - c)
    w_wait(0, c)
    give_sibling(0, 0, 0, columns)
    res_copy.wait()
    base[...] = product(0, c, 0, columns) + res_buf[...].astype(jnp.float32)

    def pos_done(i, _):
        pos_copy(i).wait_send()
        return 0

    lax.fori_loop(1, n_ctx, pos_done, 0)

    @pl.when(crossed)
    def _():
        for h in range(heads):
            for j, (src, dst) in enumerate(init_pairs(h)):
                remote(src, dst, init_send.at[h, j], init_recv.at[h, j], partner).wait_send()

            @pl.when(jnp.logical_not(left_out(h)))
            def _():
                o_copy(h, 0).wait_send()

        for j, (src, dst) in enumerate(small_pairs):
            remote(src, dst, small_send.at[j], small_recv.at[j], partner).wait_send()

    @pl.when(helper)
    def _():
        o_copy(max(off, 0), 1).wait_send()

    @pl.when(at_end)
    def _():
        q_copy().wait_send()

    def line_done(idx, _):
        for h in range(heads):

            @pl.when(jnp.logical_not(left_out(h)))
            def _():
                sib_copy(h, idx).wait_send()

        return 0

    lax.fori_loop(0, W, line_done, 0)

    def piece_done(t, _):
        for way in range(2):
            h, idx, there = piece(way, t)

            @pl.when(there & jnp.logical_not(piece(way, t + 2)[2]))
            def _():
                line_copy(h, idx, way).wait_send()

        return 0

    lax.fori_loop(0, W * heads, piece_done, 0)

    ps_copy(0, 0, 0, columns).wait()
    for i in range(1, X):
        for j, (lo, hi) in enumerate(cuts):
            ps_copy(i, j, lo, hi).wait_send()
    for j, (lo, hi) in enumerate(cuts):
        result = base[:, lo:hi] + got_sib[0, :, lo:hi].astype(jnp.float32)
        for i in range(1, X):
            p_copy(i, j).wait()
            result = result + got[i - 1, :, lo:hi].astype(jnp.float32)
        out_ref[:, lo:hi] = result.astype(out_ref.dtype)


def per_device(n_ctx, n_tp, queries, keys, values, positions, lambda_vecs, head_gain, out_weight, residual):
    rows = queries.shape[0]
    heads, depth = lambda_vecs.shape[1], lambda_vecs.shape[2]
    wide = 2 * depth
    W, X = n_ctx // 2, n_tp // 2
    columns = out_weight.shape[1] // n_tp
    n_cut = len(column_cuts(columns))
    vmem = pl.BlockSpec(memory_space=pltpu.VMEM)
    hbm = pl.BlockSpec(memory_space=pl.ANY)
    bf16, f32 = jnp.bfloat16, jnp.float32
    dma = pltpu.SemaphoreType.DMA
    return pl.pallas_call(
        functools.partial(layer_kernel, n_ctx, n_tp),
        out_shape=jax.ShapeDtypeStruct((rows, columns), bf16),
        in_specs=[hbm] * 8,
        out_specs=vmem,
        scratch_shapes=[
            pltpu.VMEM((heads + 1, rows, wide), bf16),
            pltpu.VMEM((heads, W, 2, rows, 2 * wide), bf16),
            pltpu.VMEM((n_ctx, 1, rows), jnp.int32),
            pltpu.VMEM((heads, 4, depth), f32),
            pltpu.VMEM((2 * heads, depth), f32),
            pltpu.VMEM((heads, 1, wide), f32),
            pltpu.VMEM((heads, 1, wide), f32),
            pltpu.VMEM((2, rows, 2 * rows), jnp.int32),
            pltpu.VMEM((heads + 1, 2, rows, 128), f32),
            pltpu.VMEM((heads + 1, 2, rows, 128), f32),
            pltpu.VMEM((heads + 1, 2, rows, wide), f32),
            pltpu.VMEM((heads + 1, rows, wide), bf16),
            pltpu.VMEM((rows, heads * wide), bf16),
            pltpu.VMEM((n_tp, heads * wide, columns), bf16),
            pltpu.VMEM((rows, columns), bf16),
            pltpu.VMEM((rows, columns), f32),
            pltpu.VMEM((X, rows, columns), bf16),
            pltpu.VMEM((X, rows, columns), bf16),
            pltpu.VMEM((X - 1, rows, columns), bf16),
            pltpu.VMEM((X - 1, rows, columns), bf16),
            dma((heads, 3)),
            dma((heads, 3)),
            dma((2,)),
            dma((2,)),
            dma((n_ctx,)),
            dma((n_ctx,)),
            dma((2, heads, W)),
            dma((heads, W)),
            dma((heads, W)),
            dma((heads, W)),
            dma(()),
            dma(()),
            dma((heads + 1,)),
            dma((heads,)),
            dma((n_tp,)),
            dma(()),
            dma((X, n_cut)),
            dma((X, n_cut)),
            dma((X - 1, n_cut)),
            dma((X - 1, n_cut)),
        ],
        compiler_params=pltpu.CompilerParams(
            collective_id=0, has_side_effects=True, vmem_limit_bytes=56 * 1024 * 1024
        ),
        name="attend_and_project",
    )(
        queries,
        keys,
        values,
        positions.reshape(1, rows),
        jnp.transpose(lambda_vecs, (1, 0, 2)),
        head_gain.reshape(2 * heads, depth),
        out_weight,
        residual,
    )


def solution(mesh):
    placed = (
        P("ctx", "tp"),
        P("ctx", "tp"),
        P("ctx", "tp"),
        P("ctx"),
        P(None, "tp", None),
        P("tp"),
        P("tp", None),
        P("ctx", "tp"),
    )
    return jax.shard_map(
        functools.partial(per_device, mesh.shape["ctx"], mesh.shape["tp"]),
        mesh=mesh,
        in_specs=placed,
        out_specs=P("ctx", "tp"),
        check_vma=False,
    )
```

```python
import functools
import math

import jax
import jax.numpy as jnp
from jax import lax
from jax.experimental import pallas as pl
from jax.experimental.pallas import tpu as pltpu
from jax.sharding import PartitionSpec as P

lambda_init = 0.2
out_factor = 0.8
norm_eps = 1e-05
MASKED = -3e38
LOWEST = -1e30


def column_cuts(columns):
    edges = [0] + list(range(256, columns, 512)) + [columns]
    return list(zip(edges[:-1], edges[1:]))


def layer_kernel(
    n_ctx,
    n_tp,
    q_in,
    k_in,
    v_in,
    pos_in,
    lam_in,
    gain_in,
    w_in,
    res_in,
    out_ref,
    q_buf,
    kv_buf,
    pos_all,
    lam_buf,
    gain_buf,
    lam_wide,
    gain_wide,
    q_pos,
    high,
    total,
    acc,
    stage,
    normed,
    w_buf,
    res_buf,
    base,
    part_sib,
    got_sib,
    part,
    got,
    init_send,
    init_recv,
    small_send,
    small_recv,
    pos_send,
    pos_recv,
    line_send,
    line_recv,
    sib_send,
    sib_recv,
    q_send,
    q_recv,
    o_send,
    o_recv,
    w_sem,
    res_sem,
    ps_send,
    ps_recv,
    p_send,
    p_recv,
):
    heads, rows, wide = stage.shape
    heads -= 1
    depth = wide // 2
    W = n_ctx // 2
    X = n_tp // 2
    columns = w_buf.shape[2]
    cuts = column_cuts(columns)
    off = heads - 1 if W >= 4 else -1
    scale = math.log2(math.e) / math.sqrt(depth)
    ctx = lax.axis_index("ctx")
    tp = lax.axis_index("tp")
    w, y = lax.div(ctx, 2), lax.rem(ctx, 2)
    x, c = lax.div(tp, 2), lax.rem(tp, 2)
    crossed = c != y
    straight = c == y
    at_end = (off >= 0) & ((w == 0) | (w == W - 1))
    helper = (off >= 0) & ((w == 1) | (w == W - 2))
    mate = jnp.where(w == 0, 1, jnp.where(w == W - 1, W - 2, jnp.where(w == 1, 0, jnp.where(w == W - 2, W - 1, w))))

    def left_out(h):
        return at_end & (h == off)

    def goes(way, h):
        if way:
            return (w < W - 1) & ((w != W - 2) | (h != off))
        return (w > 0) & ((w != 1) | (h != off))

    def slots(h):
        return 1 + jnp.where(helper & (h == off), 1, 0)

    def dev(a, b):
        return {"ctx": a, "tp": b}

    def remote(src, dst, send, recv, to):
        return pltpu.make_async_remote_copy(
            src_ref=src, dst_ref=dst, send_sem=send, recv_sem=recv, device_id=to, device_id_type=pl.DeviceIdType.MESH
        )

    partner = dev(2 * w + c, 2 * x + y)
    sibling = dev(ctx, 2 * x + 1 - c)
    far = dev(2 * mate + c, 2 * x + y)

    def init_pairs(h):
        cols = pl.ds(h * wide, wide)
        return (
            (k_in.at[:, cols], kv_buf.at[h, w, y, :, pl.ds(0, wide)]),
            (v_in.at[:, cols], kv_buf.at[h, w, y, :, pl.ds(wide, wide)]),
            (q_in.at[:, cols], q_buf.at[h]),
        )

    small_pairs = ((lam_in, lam_buf), (gain_in, gain_buf))

    def w_copy(i):
        start = pl.multiple_of(i * columns, 128)
        return pltpu.make_async_copy(w_in.at[:, pl.ds(start, columns)], w_buf.at[i], w_sem.at[i])

    res_copy = pltpu.make_async_copy(res_in, res_buf, res_sem)

    @pl.when(straight)
    def _():
        for h in range(heads):
            for j, (src, dst) in enumerate(init_pairs(h)):
                pltpu.make_async_copy(src, dst, init_recv.at[h, j]).start()
        for j, (src, dst) in enumerate(small_pairs):
            pltpu.make_async_copy(src, dst, small_recv.at[j]).start()

    pltpu.make_async_copy(pos_in, pos_all.at[ctx], pos_recv.at[ctx]).start()
    for k in range(2 * X):
        w_copy(2 * lax.rem(x + k // 2 + 1, X) + lax.rem(c + k + 1, 2)).start()
    res_copy.start()

    barrier = pltpu.get_barrier_semaphore()

    def greet(to):
        pl.semaphore_signal(barrier, inc=1, device_id=to, device_id_type=pl.DeviceIdType.MESH)

    greet(sibling)

    @pl.when(crossed)
    def _():
        greet(partner)

    @pl.when(crossed & (at_end | helper))
    def _():
        greet(far)

    for i in range(1, X):
        greet(dev(ctx, 2 * lax.rem(x + i, X) + c))

    def greet_row(i, _):
        greet(dev(lax.rem(ctx + i, n_ctx), tp))
        return 0

    lax.fori_loop(1, n_ctx, greet_row, 0)
    pl.semaphore_wait(barrier, n_ctx - 1 + 1 + X - 1 + lax.rem(c + y, 2) + jnp.where(crossed & (at_end | helper), 1, 0))

    def init_start(h):
        @pl.when(crossed)
        def _():
            for j, (src, dst) in enumerate(init_pairs(h)):
                remote(src, dst, init_send.at[h, j], init_recv.at[h, j], partner).start()

    for h in range(min(2, heads)):
        init_start(h)

    @pl.when(crossed)
    def _():
        for j, (src, dst) in enumerate(small_pairs):
            remote(src, dst, small_send.at[j], small_recv.at[j], partner).start()

    def pos_copy(i):
        return remote(
            pos_in,
            pos_all.at[ctx],
            pos_send.at[i],
            pos_recv.at[ctx],
            dev(lax.rem(ctx + i, n_ctx), tp),
        )

    def pos_start(i, _):
        pos_copy(i).start()
        return 0

    lax.fori_loop(1, n_ctx, pos_start, 0)

    def line_copy(h, idx, way):
        block = kv_buf.at[h, idx, c]
        to = dev(ctx + (2 if way else -2), tp)
        return remote(block, block, line_send.at[way, h, idx], line_recv.at[h, idx], to)

    def piece(way, t):
        s, h = lax.div(t + heads, heads) - 1, lax.rem(t + heads, heads)
        idx = w - s if way else w + s
        return h, idx, (s >= 0) & (idx >= 0) & (idx < W) & goes(way, h)

    def pace(way, t):
        h, idx, there = piece(way, t - 3)

        @pl.when(there)
        def _():
            line_copy(h, idx, way).wait_send()

    def sib_copy(h, idx):
        block = kv_buf.at[h, idx, c]
        return remote(block, block, sib_send.at[h, idx], sib_recv.at[h, idx], sibling)

    def sib_wait(h, idx):
        block = kv_buf.at[h, idx, 1 - c]
        remote(block, block, sib_send.at[h, idx], sib_recv.at[h, idx], sibling).wait_recv()

    def q_copy():
        return remote(q_buf.at[max(off, 0)], q_buf.at[heads], q_send, q_recv, dev(2 * mate + y, tp))

    def position_column(row):
        line = pos_all[row]
        square = (rows, rows)
        same = lax.broadcasted_iota(jnp.int32, square, 0) == lax.broadcasted_iota(jnp.int32, square, 1)
        return jnp.sum(jnp.where(same, jnp.broadcast_to(line, square), 0), -1, keepdims=True)

    def attend(h, blocks, last):
        def one(turn, _):
            k = slots(h) - 1 - turn
            e = h + k * (heads - h)
            allowed = [
                jnp.concatenate([pos_all[2 * idx], pos_all[2 * idx + 1]], axis=1) <= q_pos[k] for idx in blocks
            ]
            values = [kv_buf[h, idx, :, :, pl.ds(wide, wide)].reshape(2 * rows, wide) for idx in blocks]
            fresh = []
            for a in range(2):
                query = q_buf[e, :, pl.ds(a * depth, depth)]
                scores = []
                for idx, mask in zip(blocks, allowed):
                    key = kv_buf[h, idx, :, :, pl.ds(a * depth, depth)].reshape(2 * rows, depth)
                    raw = lax.dot_general(
                        query, key, (((1,), (1,)), ((), ())), preferred_element_type=jnp.float32
                    )
                    scores.append(jnp.where(mask, raw, MASKED))
                before = high[e, a]
                now = before
                for part_scores in scores:
                    now = jnp.maximum(now, jnp.max(part_scores, -1, keepdims=True))
                keep = jnp.exp2((before - now) * scale)
                sums = total[e, a] * keep
                held = acc[e, a] * jnp.concatenate([keep] * (wide // 128), axis=1)
                for part_scores, value in zip(scores, values):
                    expo = jnp.exp2((part_scores - now[:, :1]) * scale)
                    sums = sums + jnp.sum(expo, -1, keepdims=True)
                    held = held + jnp.dot(expo.astype(jnp.bfloat16), value, preferred_element_type=jnp.float32)
                fresh.append((now, sums, held))
            for a in range(2):
                high[e, a], total[e, a], acc[e, a] = fresh[a]

            @pl.when(last)
            def _():
                finish(h, k)

            return 0

        lax.fori_loop(0, slots(h), one, 0)

    def head_columns(h):
        return pl.ds(pl.multiple_of(h * wide, wide), wide)

    def o_copy(h, k):
        e = h + k * (heads - h)
        to = dev(2 * (w + k * (mate - w)) + c, 2 * x + y)
        return remote(stage.at[e], normed.at[:, head_columns(h)], o_send.at[e], o_recv.at[h], to)

    def finish(h, k):
        e = h + k * (heads - h)
        first = acc[e, 0] / total[e, 0, :, :1]
        second = acc[e, 1] / total[e, 1, :, :1]
        diff = first - lam_wide[h] * second
        mean_square = jnp.mean(diff * diff, -1, keepdims=True)
        result = (out_factor * diff * lax.rsqrt(mean_square + norm_eps) * gain_wide[h]).astype(jnp.bfloat16)

        @pl.when(straight & (k == 0))
        def _():
            normed[:, head_columns(h)] = result

        @pl.when(crossed | (k > 0))
        def _():
            stage[e] = result
            o_copy(h, k).start()

    high[...] = jnp.full(high.shape, LOWEST, jnp.float32)
    total[...] = jnp.zeros(total.shape, jnp.float32)
    acc[...] = jnp.zeros(acc.shape, jnp.float32)

    def step(t, _):
        s, h = lax.div(t, heads), lax.rem(t, heads)

        @pl.when(s == 0)
        def _():
            for way in range(2):

                @pl.when(straight & goes(way, h))
                def _():
                    pace(way, t)
                    to = dev(ctx + (2 if way else -2), tp)
                    own = pl.ds(pl.multiple_of(h * wide, wide), wide)
                    for j, src in enumerate((k_in, v_in)):
                        dst = kv_buf.at[h, w, y, :, pl.ds(j * wide, wide)]
                        remote(src.at[:, own], dst, line_send.at[way, h, w], line_recv.at[h, w], to).start()

            cols = pl.ds(0, wide)
            src = k_in.at[:, cols]
            pltpu.make_async_copy(src, kv_buf.at[h, w, c, :, cols], init_recv.at[h, 0]).wait()
            pltpu.make_async_copy(src, kv_buf.at[h, w, c, :, pl.ds(wide, wide)], init_recv.at[h, 1]).wait()

            for way in range(2):

                @pl.when(crossed & goes(way, h))
                def _():
                    pace(way, t)
                    line_copy(h, w, way).start()

            @pl.when(jnp.logical_not(left_out(h)))
            def _():
                sib_copy(h, w).start()

            pltpu.make_async_copy(src, q_buf.at[h], init_recv.at[h, 2]).wait()
            for later in range(2, heads):

                @pl.when(h == later - 2)
                def _():
                    init_start(later)

            @pl.when(left_out(h))
            def _():
                q_copy().start()

        @pl.when(t == heads)
        def _():
            for j, (src, dst) in enumerate(small_pairs):
                pltpu.make_async_copy(src, dst, small_recv.at[j]).wait()
            vecs = lam_buf[...]
            lam = (
                jnp.exp(jnp.sum(vecs[:, 0] * vecs[:, 1], -1, keepdims=True))
                - jnp.exp(jnp.sum(vecs[:, 2] * vecs[:, 3], -1, keepdims=True))
                + lambda_init
            )
            for i in range(heads):
                lam_wide[i] = jnp.broadcast_to(lam[i : i + 1], (1, wide))
                gain_wide[i] = jnp.concatenate([gain_buf[pl.ds(2 * i, 1)], gain_buf[pl.ds(2 * i + 1, 1)]], axis=1)

        @pl.when((s > 0) & (s < W) & jnp.logical_not(left_out(h)))
        def _():
            for way, idx in ((1, w - s), (0, w + s)):

                @pl.when((idx >= 0) & (idx < W))
                def _():
                    line_copy(h, idx, way).wait_recv()
                    sib_copy(h, idx).start()

            for way, idx in ((1, w - s), (0, w + s)):

                @pl.when((idx >= 0) & (idx < W) & goes(way, h))
                def _():
                    pace(way, t)
                    line_copy(h, idx, way).start()

        @pl.when(t == 1)
        def _():
            def pos_wait(i, _):
                frm = lax.rem(ctx + i, n_ctx)
                remote(pos_in, pos_all.at[frm], pos_send.at[i], pos_recv.at[frm], sibling).wait_recv()
                return 0

            pltpu.make_async_copy(pos_in, pos_all.at[ctx], pos_recv.at[ctx]).wait()
            lax.fori_loop(1, n_ctx, pos_wait, 0)
            q_pos[0] = jnp.broadcast_to(position_column(2 * w + c), q_pos.shape[1:])
            q_pos[1] = jnp.broadcast_to(position_column(2 * mate + c), q_pos.shape[1:])

        s1, h1 = lax.div(t + heads - 1, heads) - 1, lax.rem(t + heads - 1, heads)

        @pl.when((t > 0) & jnp.logical_not(left_out(h1)))
        def _():
            @pl.when(helper & (t == off + 1))
            def _():
                q_copy().wait_recv()

            last = s1 == jnp.maximum(w, W - 1 - w)
            on_left, on_right = w - s1 >= 0, (s1 > 0) & (w + s1 < W)

            @pl.when(on_left & on_right)
            def _():
                sib_wait(h1, w - s1)
                sib_wait(h1, w + s1)
                attend(h1, (w - s1, w + s1), last)

            @pl.when(on_left != on_right)
            def _():
                idx = jnp.where(on_left, w - s1, w + s1)
                sib_wait(h1, idx)
                attend(h1, (idx,), last)

        return 0

    lax.fori_loop(0, W * heads + 1, step, 0)

    for h in range(heads):

        @pl.when(crossed | left_out(h))
        def _():
            o_copy(h, 0).wait_recv()

    def product(i, core, lo, hi):
        target = 2 * lax.rem(x + i, X) + core
        return jnp.dot(normed[...], w_buf[target, :, lo:hi], preferred_element_type=jnp.float32)

    def w_wait(i, core):
        w_copy(2 * lax.rem(x + i, X) + core).wait()

    def ps_copy(i, j, lo, hi):
        cols = pl.ds(lo, hi - lo)
        return remote(part_sib.at[i, :, cols], got_sib.at[i, :, cols], ps_send.at[i, j], ps_recv.at[i, j], sibling)

    def p_copy(i, j):
        lo, hi = cuts[j]
        cols = pl.ds(lo, hi - lo)
        to = dev(ctx, 2 * lax.rem(x + i, X) + c)
        return remote(
            part.at[i - 1, :, cols], got.at[i - 1, :, cols], p_send.at[i - 1, j], p_recv.at[i - 1, j], to
        )

    def give_sibling(i, j, lo, hi):
        part_sib[i, :, lo:hi] = product(i, 1 - c, lo, hi).astype(jnp.bfloat16)
        ps_copy(i, j, lo, hi).start()

    for i in range(1, X):
        w_wait(i, 1 - c)
        w_wait(i, c)
        for j in range(len(cuts) + 1):
            if j < len(cuts):
                give_sibling(i, j, *cuts[j])
            if j >= 1:
                lo, hi = cuts[j - 1]
                mine = product(i, c, lo, hi)
                ps_copy(i, j - 1, lo, hi).wait_recv()
                part[i - 1, :, lo:hi] = (mine + got_sib[i, :, lo:hi].astype(jnp.float32)).astype(jnp.bfloat16)
                p_copy(i, j - 1).start()
    w_wait(0, 1 - c)
    w_wait(0, c)
    give_sibling(0, 0, 0, columns)
    res_copy.wait()
    base[...] = product(0, c, 0, columns) + res_buf[...].astype(jnp.float32)

    def pos_done(i, _):
        pos_copy(i).wait_send()
        return 0

    lax.fori_loop(1, n_ctx, pos_done, 0)

    @pl.when(crossed)
    def _():
        for h in range(heads):
            for j, (src, dst) in enumerate(init_pairs(h)):
                remote(src, dst, init_send.at[h, j], init_recv.at[h, j], partner).wait_send()

            @pl.when(jnp.logical_not(left_out(h)))
            def _():
                o_copy(h, 0).wait_send()

        for j, (src, dst) in enumerate(small_pairs):
            remote(src, dst, small_send.at[j], small_recv.at[j], partner).wait_send()

    @pl.when(helper)
    def _():
        o_copy(max(off, 0), 1).wait_send()

    @pl.when(at_end)
    def _():
        q_copy().wait_send()

    def line_done(idx, _):
        for h in range(heads):

            @pl.when(jnp.logical_not(left_out(h)))
            def _():
                sib_copy(h, idx).wait_send()

        return 0

    lax.fori_loop(0, W, line_done, 0)

    def piece_done(t, _):
        for way in range(2):
            h, idx, there = piece(way, t)

            @pl.when(there & jnp.logical_not(piece(way, t + 3)[2]))
            def _():
                line_copy(h, idx, way).wait_send()

        return 0

    lax.fori_loop(0, W * heads, piece_done, 0)

    ps_copy(0, 0, 0, columns).wait()
    for i in range(1, X):
        for j, (lo, hi) in enumerate(cuts):
            ps_copy(i, j, lo, hi).wait_send()
    for j, (lo, hi) in enumerate(cuts):
        result = base[:, lo:hi] + got_sib[0, :, lo:hi].astype(jnp.float32)
        for i in range(1, X):
            p_copy(i, j).wait()
            result = result + got[i - 1, :, lo:hi].astype(jnp.float32)
        out_ref[:, lo:hi] = result.astype(out_ref.dtype)


def per_device(n_ctx, n_tp, queries, keys, values, positions, lambda_vecs, head_gain, out_weight, residual):
    rows = queries.shape[0]
    heads, depth = lambda_vecs.shape[1], lambda_vecs.shape[2]
    wide = 2 * depth
    W, X = n_ctx // 2, n_tp // 2
    columns = out_weight.shape[1] // n_tp
    n_cut = len(column_cuts(columns))
    vmem = pl.BlockSpec(memory_space=pltpu.VMEM)
    hbm = pl.BlockSpec(memory_space=pl.ANY)
    bf16, f32 = jnp.bfloat16, jnp.float32
    dma = pltpu.SemaphoreType.DMA
    return pl.pallas_call(
        functools.partial(layer_kernel, n_ctx, n_tp),
        out_shape=jax.ShapeDtypeStruct((rows, columns), bf16),
        in_specs=[hbm] * 8,
        out_specs=vmem,
        scratch_shapes=[
            pltpu.VMEM((heads + 1, rows, wide), bf16),
            pltpu.VMEM((heads, W, 2, rows, 2 * wide), bf16),
            pltpu.VMEM((n_ctx, 1, rows), jnp.int32),
            pltpu.VMEM((heads, 4, depth), f32),
            pltpu.VMEM((2 * heads, depth), f32),
            pltpu.VMEM((heads, 1, wide), f32),
            pltpu.VMEM((heads, 1, wide), f32),
            pltpu.VMEM((2, rows, 2 * rows), jnp.int32),
            pltpu.VMEM((heads + 1, 2, rows, 128), f32),
            pltpu.VMEM((heads + 1, 2, rows, 128), f32),
            pltpu.VMEM((heads + 1, 2, rows, wide), f32),
            pltpu.VMEM((heads + 1, rows, wide), bf16),
            pltpu.VMEM((rows, heads * wide), bf16),
            pltpu.VMEM((n_tp, heads * wide, columns), bf16),
            pltpu.VMEM((rows, columns), bf16),
            pltpu.VMEM((rows, columns), f32),
            pltpu.VMEM((X, rows, columns), bf16),
            pltpu.VMEM((X, rows, columns), bf16),
            pltpu.VMEM((X - 1, rows, columns), bf16),
            pltpu.VMEM((X - 1, rows, columns), bf16),
            dma((heads, 3)),
            dma((heads, 3)),
            dma((2,)),
            dma((2,)),
            dma((n_ctx,)),
            dma((n_ctx,)),
            dma((2, heads, W)),
            dma((heads, W)),
            dma((heads, W)),
            dma((heads, W)),
            dma(()),
            dma(()),
            dma((heads + 1,)),
            dma((heads,)),
            dma((n_tp,)),
            dma(()),
            dma((X, n_cut)),
            dma((X, n_cut)),
            dma((X - 1, n_cut)),
            dma((X - 1, n_cut)),
        ],
        compiler_params=pltpu.CompilerParams(
            collective_id=0, has_side_effects=True, vmem_limit_bytes=56 * 1024 * 1024
        ),
        name="attend_and_project",
    )(
        queries,
        keys,
        values,
        positions.reshape(1, rows),
        jnp.transpose(lambda_vecs, (1, 0, 2)),
        head_gain.reshape(2 * heads, depth),
        out_weight,
        residual,
    )


def solution(mesh):
    placed = (
        P("ctx", "tp"),
        P("ctx", "tp"),
        P("ctx", "tp"),
        P("ctx"),
        P(None, "tp", None),
        P("tp"),
        P("tp", None),
        P("ctx", "tp"),
    )
    return jax.shard_map(
        functools.partial(per_device, mesh.shape["ctx"], mesh.shape["tp"]),
        mesh=mesh,
        in_specs=placed,
        out_specs=P("ctx", "tp"),
        check_vma=False,
    )
```
